32 devices in a mesh: group: 2 (over x), dom: 16 (over z, y, core).
Axes of the slice: x: 2, y: 2, z: 4, core: 2. Of those that a mesh axis runs over, the one named last changes fastest.
Arguments:
- matrices: bfloat16 [4, 768, 6, 128, 128], P(None, ('group', 'dom')), parts along dimension 1, may hold values from -0.21875 to 0.21875
- values: bfloat16 [98304, 256], P(('group', 'dom')), parts along dimension 0, may hold values from -6 to 6
- exponents: int32 [768], P(('group', 'dom')), parts along dimension 0, may hold values from -2 to 2
- pattern: int32 [4, 768, 6], P(None, ('group', 'dom')), parts along dimension 1, may hold values from 0 to 87, as said below
- block_counts: int32 [4, 768], P(None, ('group', 'dom')), parts along dimension 1, may hold values from 1 to 6
- send_lists: int32 [32, 16, 4], P(('group', 'dom')), parts along dimension 0, may hold values from 0 to 23, as said below
- ghost_counts: int32 [32, 16], P(('group', 'dom')), parts along dimension 0, may hold values from 0 to 4, as said below
Outputs:
- reduced: float32 [2048, 256], P(('group', 'dom')), parts along dimension 0
The draws below stay inside these ranges and needn't reach their ends.
There are 2 independent parts, one for each index of `group`. The reference program is written for one: setup_inputs(seed, part) draws one part's arguments, and reference() takes and returns one part's arrays. A program takes and returns all parts, laid end to end along the dimension named above; each array names one. Nothing has to cross between parts.
Inputs may be any that keep to these rules, and one draw needn't show every extreme that they name: `pattern`: every entry names a slot below 24 (an own block) or 24 + p * 4 + g with g below ghost_counts[p, d] for the partition d that holds the row; slot k = 0 is the row block's own diagonal block. `send_lists`: the 4 entries of one pair are distinct. `ghost_counts`: zero for a partition and itself; at most 1 for partitions p, r with |p - r| other than 1; at least 1 for adjacent partitions.
All inputs are finite; a program needn't handle non-finite values.
Results may differ from the reference program's by a relative error of at most 0.0029.
Values may be sent and summed in bfloat16 or wider, within the bound.
No kernel may reach another device: no remote copies, remote signals or barrier semaphores. Data moves between devices by JAX's collectives and lax.ppermute only.
A program may use at most 192 MiB of HBM per device.

```python
import math
import jax
import jax.numpy as jnp
from jax import lax

BS = 128
R = 256
Q = 4
K = 6
ROWB = 24
GHOST = 4
GHOST_FAR = 1
DOMAINS = 16
BLOCKS = 384
NROWS = 49152


def ghost_table(key):
    sender = jnp.arange(DOMAINS)[:, None]
    taker = jnp.arange(DOMAINS)[None, :]
    distance = jnp.abs(sender - taker)
    adjacent = jax.random.randint(key, (DOMAINS, DOMAINS), 1, GHOST + 1)
    distant = jax.random.randint(jax.random.fold_in(key, 1), (DOMAINS, DOMAINS), 0, GHOST_FAR + 1)
    table = jnp.where(distance == 1, adjacent, jnp.where(distance == 0, 0, distant))
    opposite = sender == (taker + DOMAINS // 2) % DOMAINS
    table = jnp.where(opposite, GHOST_FAR, table)
    table = jnp.where((sender == DOMAINS - 1) & (taker == DOMAINS - 2), GHOST, table)
    table = jnp.where((sender == 0) & (taker == 1), GHOST, table)
    table = jnp.where((sender == 0) & (taker == DOMAINS - 1), GHOST_FAR, table)
    return table.astype(jnp.int32)


def draw_ghost_counts(key, part):
    return ghost_table(key)


def draw_pattern(key, part):
    lending = ghost_table(key)
    key = jax.random.fold_in(key, 21)
    keys = jax.random.split(key, 4)
    shape = (Q, BLOCKS, K)
    block_ids = jnp.arange(BLOCKS)[None, :, None] + jnp.zeros(shape, jnp.int32)
    device_of = block_ids // ROWB
    slot_ids = jnp.arange(K)[None, None, :] + jnp.zeros(shape, jnp.int32)
    own_slot = jax.random.randint(keys[0], shape, 0, ROWB)
    choose = jax.random.randint(keys[1], shape, 0, 10)
    distant = jax.random.randint(keys[2], shape, 0, DOMAINS)
    sender = jnp.where(choose < 8, device_of - 1, jnp.where(choose < 9, device_of + 1, distant))
    inside = (sender >= 0) & (sender < DOMAINS) & (choose >= 6)
    sender_safe = jnp.clip(sender, 0, DOMAINS - 1)
    lent = lending[sender_safe, device_of]
    raw_bits = jax.random.randint(keys[3], shape, 0, 65536)
    within = raw_bits % jnp.maximum(lent, 1)
    usable = inside & (lent > 0)
    slot = jnp.where(usable, ROWB + sender_safe * GHOST + within, own_slot)
    slot = jnp.where(slot_ids == 0, block_ids % ROWB, slot)
    opposite = (device_of + DOMAINS // 2) % DOMAINS
    slot = jnp.where((block_ids % ROWB == 0) & (slot_ids == 1), ROWB + opposite * GHOST, slot)
    forced_block = (DOMAINS - 1) * ROWB - 1
    slot = jnp.where((block_ids == forced_block) & (slot_ids == 1), ROWB + DOMAINS * GHOST - 1, slot)
    return slot.astype(jnp.int32)


def draw_block_counts(key, part):
    key = jax.random.fold_in(key, 22)
    first, second = jax.random.split(key)
    density = jax.random.randint(first, (1, DOMAINS, 1), 2, K + 1)
    raw_bits = jax.random.randint(second, (Q, DOMAINS, ROWB), 0, 65536)
    counts = (1 + raw_bits % density).reshape(Q, BLOCKS)
    block_ids = jnp.arange(BLOCKS)[None, :]
    counts = jnp.where(block_ids % ROWB == 0, jnp.maximum(counts, 2), counts)
    counts = jnp.where(block_ids == (DOMAINS - 1) * ROWB - 1, K, counts)
    return counts.astype(jnp.int32)


def draw_send_lists(key, part):
    key = jax.random.fold_in(key, 23)
    offsets = jax.random.randint(key, (DOMAINS, DOMAINS, 1), 0, ROWB)
    first_pair = (jnp.arange(DOMAINS)[:, None, None] == 0) & (jnp.arange(DOMAINS)[None, :, None] == 0)
    offsets = jnp.where(first_pair, ROWB - 1, offsets)
    return ((offsets + jnp.arange(GHOST)[None, None, :]) % ROWB).astype(jnp.int32)


def plant(drawn, key, low, largest):
    spot = [jax.random.randint(jax.random.fold_in(key, axis), (), 0, length) for axis, length in enumerate(drawn.shape)]
    longest = drawn.shape.index(max(drawn.shape))
    beside = spot[:longest] + [(spot[longest] + 1) % drawn.shape[longest]] + spot[longest + 1:]
    return drawn.at[tuple(spot)].set(low).at[tuple(beside)].set(largest)


def levels(rng, shape, cuts, low, top_value):
    factor_of = 1.0
    for dim, blocks in cuts:
        steps = jax.random.uniform(jax.random.fold_in(jax.random.fold_in(rng, 6), dim), (blocks,), jnp.float32, low / len(cuts), top_value / len(cuts))
        factor_of = factor_of * jnp.repeat(jnp.exp(steps), shape[dim] // blocks).reshape((-1,) + (1,) * (len(shape) - 1 - dim))
    return factor_of


def normal_values(rng, extent, scale, reach, cuts=(), kind=jnp.bfloat16):
    array = jax.random.normal(rng, extent, jnp.float32) * scale
    if len(cuts) > 0:
        array = levels(rng, extent, cuts, -0.22, 0.18) * array
    return jnp.clip(array, min=-reach, max=reach).astype(kind)


def setup_inputs(seed: int = 0, part: int = 0) -> dict:
    splits = jax.random.split(jax.random.key(seed), 8)
    own_keys = jax.random.split(jax.random.fold_in(splits[7], part), 8)
    matrices = normal_values(own_keys[0], (Q, BLOCKS, K, BS, BS), (BS * K) ** -0.5, 0.21875, ((1, 16),))
    values = normal_values(own_keys[1], (NROWS, R), 1.0, 6.0, ((0, 16),))
    exponents = plant(jax.random.randint(own_keys[2], (BLOCKS,), -2, 3), jax.random.fold_in(own_keys[2], 1), -2, 2).astype(jnp.int32)
    pattern = draw_pattern(jax.random.fold_in(jax.random.fold_in(splits[7], part), 71), part)
    block_counts = draw_block_counts(jax.random.fold_in(jax.random.fold_in(splits[7], part), 71), part)
    send_lists = draw_send_lists(jax.random.fold_in(jax.random.fold_in(splits[7], part), 71), part)
    ghost_counts = draw_ghost_counts(jax.random.fold_in(jax.random.fold_in(splits[7], part), 71), part)
    return dict(matrices=matrices, values=values, exponents=exponents, pattern=pattern, block_counts=block_counts, send_lists=send_lists, ghost_counts=ghost_counts)


def reference(matrices, values, exponents, pattern, block_counts, send_lists, ghost_counts):
    factor = jnp.exp2(exponents.astype(jnp.float32)).astype(jnp.bfloat16)
    scaled = values.reshape(BLOCKS, BS, R) * factor[:, None, None]
    slot_steps = jnp.arange(K, dtype=jnp.int32)
    lend_steps = jnp.arange(GHOST, dtype=jnp.int32)
    partition_ids = jnp.arange(DOMAINS, dtype=jnp.int32)

    def partition(device):
        start = (device * ROWB).astype(jnp.int32)
        owned_blocks = lax.dynamic_slice_in_dim(scaled, start, ROWB, 0)
        listed = send_lists[:, device, :]
        sources = partition_ids[:, None] * ROWB + listed
        ghost_blocks = scaled[sources.reshape(-1)].reshape(DOMAINS, GHOST, BS, R)
        valid = lend_steps[None, :] < ghost_counts[:, device][:, None]
        ghost_blocks = jnp.where(valid[:, :, None, None], ghost_blocks, jnp.zeros((), jnp.bfloat16))
        lookup = jnp.concatenate([owned_blocks, ghost_blocks.reshape(DOMAINS * GHOST, BS, R)], 0)
        local_mats = lax.dynamic_slice_in_dim(matrices, start, ROWB, 1)
        slots = lax.dynamic_slice_in_dim(pattern, start, ROWB, 1)
        counts = lax.dynamic_slice_in_dim(block_counts, start, ROWB, 1)
        gathered = lookup[slots.reshape(-1)].reshape(Q, ROWB, K, BS, R)
        present = slot_steps[None, None, :] < counts[:, :, None]
        gathered = jnp.where(present[:, :, :, None, None], gathered, jnp.zeros((), jnp.bfloat16))
        product = jnp.einsum('qbkij,qbkjr->qbir', local_mats.astype(jnp.float32), gathered.astype(jnp.float32), precision=lax.Precision.HIGHEST).astype(jnp.bfloat16)
        return jnp.einsum('bir,qbis->qrs', owned_blocks.astype(jnp.float32), product.astype(jnp.float32), precision=lax.Precision.HIGHEST)
    partials = lax.map(partition, partition_ids)
    total = lax.optimization_barrier(jnp.sum(partials, axis=0))
    return (total * (1.0 / math.sqrt(NROWS))).reshape(Q * R, R)
```

```python
import functools
import math

import jax
import jax.numpy as jnp
from jax import lax
from jax.experimental import pallas as pl
from jax.experimental.pallas import tpu as pltpu
from jax.sharding import PartitionSpec as P

SMEM = pl.BlockSpec(memory_space=pltpu.SMEM)
HBM = pl.BlockSpec(memory_space=pl.ANY)


def power_of_two(exponent):
    return lax.shift_left(jnp.int32(1), exponent + 2).astype(jnp.float32) * 0.25


def pack_kernel(parts, size, lists, exponents, values, far, after, before, held, came, went):
    me = lax.axis_index("dom")
    lent = lists.shape[2]
    upper = jnp.minimum(me + 1, parts - 1)
    lower = jnp.maximum(me - 1, 0)
    places = [(lists[0, p, 0], far.at[p]) for p in range(parts)]
    places += [(lists[0, upper, g], after.at[g - 1]) for g in range(1, lent)]
    places += [(lists[0, lower, g], before.at[g - 1]) for g in range(1, lent)]
    incoming, outgoing = [], []
    for n, (block, place) in enumerate(places):
        rows = pl.ds(pl.multiple_of(block * size, size), size)
        incoming.append(pltpu.make_async_copy(values.at[rows, :], held.at[n], came.at[n]))
        incoming[-1].start()
    for n, (block, place) in enumerate(places):
        incoming[n].wait()
        factor = power_of_two(exponents[block]).astype(jnp.bfloat16)
        held[n] = held[n] * factor
        outgoing.append(pltpu.make_async_copy(held.at[n], place, went.at[n]))
        outgoing[-1].start()
    for copy in outgoing:
        copy.wait()


def pack(lists, exponents, values, size):
    parts, lent = lists.shape[1:]
    columns = values.shape[1]
    blocks = parts + 2 * (lent - 1)
    block = lambda n: jax.ShapeDtypeStruct((n, size, columns), values.dtype)
    return pl.pallas_call(
        functools.partial(pack_kernel, parts, size),
        out_shape=(block(parts), block(lent - 1), block(lent - 1)),
        in_specs=[SMEM, SMEM, HBM],
        out_specs=(HBM, HBM, HBM),
        scratch_shapes=[
            pltpu.VMEM((blocks, size, columns), values.dtype),
            pltpu.SemaphoreType.DMA((blocks,)),
            pltpu.SemaphoreType.DMA((blocks,)),
        ],
        name="pack",
    )(lists, exponents, values)


def project_kernel(ghosts, slots, counts, exponents, values, matrices, weights, partial, acc, basis, staged, went):
    step = pl.program_id(0)
    terms, owned, kept = slots.shape
    size, columns = values.shape

    @pl.when(step == 0)
    def _():
        def clear(n, carry):
            acc[n] = jnp.zeros(acc.shape[1:], acc.dtype)
            return carry
        lax.fori_loop(0, acc.shape[0], clear, 0)

    scaled = values[...] * power_of_two(exponents[step]).astype(jnp.bfloat16)
    basis[pl.ds(pl.multiple_of(step * size, size), size), :] = scaled
    turned = scaled.T
    for q in range(terms):
        for k in range(0, kept, 2):
            @pl.when(counts[q, step] > k)
            def _(q=q, k=k):
                pair = jnp.concatenate([matrices[q, 0, k], matrices[q, 0, k + 1]], axis=1)
                both = jnp.dot(turned, pair, preferred_element_type=jnp.float32)
                acc[slots[q, step, k]] += both[:, :size]
                acc[slots[q, step, k + 1]] += both[:, size:]

    @pl.when(step == pl.num_programs(0) - 1)
    def _():
        stride = owned + ghosts
        copies = []
        for q in range(terms):
            for g in range(ghosts):
                staged[q, :, g * size:(g + 1) * size] = acc[q * stride + owned + g].astype(jnp.bfloat16)
            copies.append(pltpu.make_async_copy(staged.at[q], weights.at[q], went.at[q]))
            copies[-1].start()

        def own(q, carry):
            total = jnp.zeros((columns, columns), jnp.float32)
            for j in range(0, owned, 2):
                exact = jnp.concatenate([acc[q * stride + j], acc[q * stride + j + 1]], axis=1)
                high = exact.astype(jnp.bfloat16)
                low = (exact - high.astype(jnp.float32)).astype(jnp.bfloat16)
                rows = basis[j * size:(j + 2) * size, :]
                total += jnp.dot(high, rows, preferred_element_type=jnp.float32)
                total += jnp.dot(low, rows, preferred_element_type=jnp.float32)
            partial[pl.ds(pl.multiple_of(q * columns, columns), columns), :] = total
            return carry

        lax.fori_loop(0, terms, own, 0)
        for copy in copies:
            copy.wait()


def project(slots, counts, exponents, values, matrices, ghosts):
    terms, owned, kept = slots.shape
    size = matrices.shape[-1]
    columns = values.shape[1]
    wide = ghosts * size
    return pl.pallas_call(
        functools.partial(project_kernel, ghosts),
        grid=(owned,),
        out_shape=(
            jax.ShapeDtypeStruct((terms, columns, wide), jnp.bfloat16),
            jax.ShapeDtypeStruct((terms * columns, columns), jnp.float32),
        ),
        in_specs=[
            SMEM,
            SMEM,
            SMEM,
            pl.BlockSpec((size, columns), lambda b: (b, 0)),
            pl.BlockSpec((terms, 1, kept, size, size), lambda b: (0, b, 0, 0, 0)),
        ],
        out_specs=(HBM, pl.BlockSpec((terms * columns, columns), lambda b: (0, 0))),
        scratch_shapes=[
            pltpu.VMEM((terms * (owned + ghosts) + 1, columns, size), jnp.float32),
            pltpu.VMEM(values.shape, values.dtype),
            pltpu.VMEM((terms, columns, wide), jnp.bfloat16),
            pltpu.SemaphoreType.DMA((terms,)),
        ],
        compiler_params=pltpu.CompilerParams(vmem_limit_bytes=56 * 2**20),
        cost_estimate=pl.CostEstimate(
            flops=2 * matrices.size * columns, bytes_accessed=2 * matrices.size, transcendentals=0
        ),
        name="project",
    )(slots, counts, exponents, values, matrices)


def finish_kernel(share, weights, far, below, above, own, keep, send):
    parity = lax.rem(lax.axis_index("dom"), 2)
    total = own[...]
    start = 0
    for blocks in (far, below, above):
        stop = start + blocks.shape[0]
        total += jnp.dot(weights[:, start:stop], blocks[...], preferred_element_type=jnp.float32)
        start = stop
    halves = total.reshape(-1, 2, share, total.shape[1])
    even = halves[:, 0].reshape(keep.shape)
    odd = halves[:, 1].reshape(keep.shape)
    keep[...] = jnp.where(parity == 0, even, odd)
    send[...] = jnp.where(parity == 0, odd, even)


def finish(weights, far, below, above, own, share, tile):
    rows, wide = weights.shape
    columns = own.shape[1]
    whole = lambda a: pl.BlockSpec(a.shape, lambda t: (0, 0))
    half = jax.ShapeDtypeStruct((rows // 2, columns), jnp.float32)
    return pl.pallas_call(
        functools.partial(finish_kernel, share),
        grid=(rows // tile,),
        out_shape=(half, half),
        in_specs=[
            pl.BlockSpec((tile, wide), lambda t: (t, 0)),
            whole(far),
            whole(below),
            whole(above),
            pl.BlockSpec((tile, columns), lambda t: (t, 0)),
        ],
        out_specs=(pl.BlockSpec((tile // 2, columns), lambda t: (t, 0)),) * 2,
        compiler_params=pltpu.CompilerParams(vmem_limit_bytes=32 * 2**20),
        name="finish",
    )(weights, far, below, above, own)


def on_device(matrices, values, exponents, pattern, block_counts, send_lists, ghost_counts):
    parts = lax.axis_size("dom")
    me = lax.axis_index("dom")
    terms, owned, kept = pattern.shape
    size = matrices.shape[-1]
    lent = send_lists.shape[2]
    row_count, columns = values.shape
    ghosts = parts + 2 * (lent - 1)

    far, after, before = pack(send_lists, exponents, values, size)
    far = lax.all_to_all(far, "dom", split_axis=0, concat_axis=0, tiled=True)
    below = lax.ppermute(after, "dom", [(p, p + 1) for p in range(parts - 1)])
    above = lax.ppermute(before, "dom", [(p + 1, p) for p in range(parts - 1)])

    ghost = pattern - owned
    lender, which = ghost // lent, ghost % lent
    further = parts + which - 1 + jnp.where(lender > me, lent - 1, 0)
    slot = jnp.where(pattern < owned, pattern, owned + jnp.where(which == 0, lender, further))
    slot = slot + (owned + ghosts) * jnp.arange(terms, dtype=jnp.int32)[:, None, None]
    present = jnp.arange(kept)[None, None, :] < block_counts[:, :, None]
    slot = jnp.where(present, slot, terms * (owned + ghosts))

    weights, own = project(slot, block_counts, exponents, values, matrices, ghosts)
    share = terms * columns // parts
    flat = lambda a: a.reshape(-1, columns)
    keep, send = finish(
        weights.reshape(terms * columns, -1), flat(far), flat(below), flat(above), own, share, max(128, 2 * share)
    )
    both = keep + lax.ppermute(send, "dom", [(p, p ^ 1) for p in range(parts)])
    both = both.astype(jnp.bfloat16).reshape(parts // 2, share, columns)
    groups = [list(range(core, parts, 2)) for core in range(2)]
    pieces = lax.all_to_all(both, "dom", split_axis=0, concat_axis=0, tiled=True, axis_index_groups=groups)
    summed = jnp.sum(pieces.astype(jnp.float32), axis=0)
    return summed * (1.0 / math.sqrt(row_count * parts))


def solution(mesh):
    return jax.shard_map(
        on_device,
        mesh=mesh,
        in_specs=(
            P(None, ("group", "dom"), None, None, None),
            P(("group", "dom"), None),
            P(("group", "dom")),
            P(None, ("group", "dom"), None),
            P(None, ("group", "dom")),
            P(("group", "dom"), None, None),
            P(("group", "dom"), None),
        ),
        out_specs=P(("group", "dom"), None),
        check_vma=False,
    )
```

```python
import functools
import math

import jax
import jax.numpy as jnp
from jax import lax
from jax.experimental import pallas as pl
from jax.experimental.pallas import tpu as pltpu
from jax.sharding import PartitionSpec as P

SMEM = pl.BlockSpec(memory_space=pltpu.SMEM)
VMEM = pl.BlockSpec(memory_space=pltpu.VMEM)
HBM = pl.BlockSpec(memory_space=pl.ANY)


def power_of_two(exponent):
    return (lax.shift_left(jnp.int32(1), exponent + 2).astype(jnp.float32) * 0.25).astype(jnp.bfloat16)


def pack_kernel(parts, size, lists, exponents, values, far, after, before):
    me = lax.axis_index("dom")
    lent = lists.shape[1]
    upper = jnp.minimum(me + 1, parts - 1)
    lower = jnp.maximum(me - 1, 0)

    def lend(block, out, n):
        rows = pl.ds(pl.multiple_of(block * size, size), size)
        out[n] = values[rows, :] * power_of_two(exponents[block])

    for p in range(parts):
        lend(lists[0, 0, p], far, p)
    for g in range(1, lent):
        lend(lists[0, g, upper], after, g - 1)
        lend(lists[0, g, lower], before, g - 1)


def pack(lists, exponents, values, size):
    lent, parts = lists.shape[1:]
    columns = values.shape[1]
    block = lambda n: jax.ShapeDtypeStruct((n, size, columns), values.dtype)
    return pl.pallas_call(
        functools.partial(pack_kernel, parts, size),
        out_shape=(block(parts), block(lent - 1), block(lent - 1)),
        in_specs=[SMEM, SMEM, VMEM],
        out_specs=(VMEM, VMEM, VMEM),
        name="pack",
    )(lists, exponents, values)


def project_kernel(
    parts, lent, pattern, counts, exponents, values, matrices, weights, partial,
    acc, basis, high, low, ring, came, terms_of, slots_of,
):
    me = lax.axis_index("dom")
    kept, terms, owned = pattern.shape
    depth = ring.shape[0]
    size = ring.shape[-1]
    columns = values.shape[1]
    ghosts = parts + 2 * (lent - 1)
    steps = owned // 2

    def fetch(step, place):
        return pltpu.make_async_copy(matrices.at[:, pl.ds(2 * step, 2)], ring.at[place], came.at[place])

    for step in range(depth):
        fetch(step, step).start()

    def clear(n, carry):
        acc[n] = jnp.zeros(acc.shape[1:], acc.dtype)
        return carry

    lax.fori_loop(0, acc.shape[0], clear, 0)

    def scale(n, carry):
        rows = pl.ds(pl.multiple_of(n * size, size), size)
        basis[n] = values[rows, :] * power_of_two(exponents[n])
        return carry

    lax.fori_loop(0, owned, scale, 0)
    basis[owned] = jnp.zeros(basis.shape[1:], basis.dtype)
    partial[...] = jnp.zeros(partial.shape, partial.dtype)

    def body(step, carry):
        place = lax.rem(step, depth)
        fetch(step, place).wait()
        rows = jnp.concatenate([basis[2 * step], basis[2 * step + 1]], axis=0)
        turned = rows.T
        listed = []
        for sub in range(2):
            b = 2 * step + sub
            found = jnp.int32(0)
            for q in range(terms):
                count = counts[q, b]
                before = found
                tables = []
                for k in range(kept):
                    slot = pattern[k, q, b]
                    present = count > k
                    tables.append(basis[jnp.where(present & (slot < owned), slot, owned)])
                    terms_of[sub, found] = q
                    slots_of[sub, found] = k
                    found += (present & (slot >= owned)).astype(jnp.int32)
                left = jnp.concatenate([ring[place, q, sub, k] for k in range(kept)], axis=1)
                exact = jnp.dot(left, jnp.concatenate(tables, axis=0), preferred_element_type=jnp.float32)
                upper = exact.astype(jnp.bfloat16)
                rest = (exact - upper.astype(jnp.float32)) * (found > before).astype(jnp.float32)
                high[q, sub * size:(sub + 1) * size, :] = upper
                low[q, sub * size:(sub + 1) * size, :] = rest.astype(jnp.bfloat16)
            listed.append(found)
        for q in range(terms):
            rows = slice(q * columns, (q + 1) * columns)
            partial[rows, :] += jnp.dot(turned, high[q], preferred_element_type=jnp.float32) + jnp.dot(
                turned, low[q], preferred_element_type=jnp.float32
            )
        for sub in range(2):
            b = 2 * step + sub
            left = turned[:, sub * size:(sub + 1) * size]

            def ghost(n, carry, sub=sub, b=b, left=left):
                def take(n):
                    real = n < listed[sub]
                    q = jnp.where(real, terms_of[sub, n], 0)
                    k = jnp.where(real, slots_of[sub, n], 0)
                    slot = pattern[k, q, b] - owned
                    lender, which = lax.div(slot, lent), lax.rem(slot, lent)
                    further = parts + which - 1 + jnp.where(lender > me, lent - 1, 0)
                    target = q * ghosts + jnp.where(which == 0, lender, further)
                    return ring[place, q, sub, k], jnp.where(real, target, terms * ghosts)

                first, first_target = take(2 * n)
                second, second_target = take(2 * n + 1)
                both = jnp.dot(left, jnp.concatenate([first, second], axis=1), preferred_element_type=jnp.float32)
                acc[first_target] += both[:, :size]
                acc[second_target] += both[:, size:]
                return carry

            lax.fori_loop(0, lax.div(listed[sub] + 1, 2), ghost, 0)

        @pl.when(step + depth < steps)
        def _():
            fetch(step + depth, place).start()

        return carry

    lax.fori_loop(0, steps, body, 0)

    def settle(q, carry):
        rows = pl.ds(pl.multiple_of(q * columns, columns), columns)
        for g in range(ghosts):
            weights[rows, g * size:(g + 1) * size] = acc[q * ghosts + g].astype(jnp.bfloat16)
        return carry

    lax.fori_loop(0, terms, settle, 0)


def project(pattern, counts, exponents, values, matrices, parts, lent):
    kept, terms, owned = pattern.shape
    size = matrices.shape[-1]
    columns = values.shape[1]
    ghosts = parts + 2 * (lent - 1)
    depth = 3
    scratch = [
        ((terms * ghosts + 1, columns, size), jnp.float32),
        ((owned + 1, size, columns), jnp.bfloat16),
        ((terms, 2 * size, columns), jnp.bfloat16),
        ((terms, 2 * size, columns), jnp.bfloat16),
        ((depth, terms, 2, kept, size, size), jnp.bfloat16),
    ]
    outs = [((terms * columns, ghosts * size), jnp.bfloat16), ((terms * columns, columns), jnp.float32)]
    needed = sum(math.prod(shape) * jnp.dtype(dtype).itemsize for shape, dtype in scratch + outs + [(values.shape, jnp.bfloat16)])
    return pl.pallas_call(
        functools.partial(project_kernel, parts, lent),
        out_shape=tuple(jax.ShapeDtypeStruct(*out) for out in outs),
        in_specs=[SMEM, SMEM, SMEM, VMEM, HBM],
        out_specs=(VMEM, VMEM),
        scratch_shapes=[pltpu.VMEM(shape, dtype) for shape, dtype in scratch] + [
            pltpu.SemaphoreType.DMA((depth,)),
            pltpu.SMEM((2, terms * kept + 1), jnp.int32),
            pltpu.SMEM((2, terms * kept + 1), jnp.int32),
        ],
        compiler_params=pltpu.CompilerParams(vmem_limit_bytes=needed + 4 * 2**20),
        cost_estimate=pl.CostEstimate(
            flops=2 * matrices.size * columns, bytes_accessed=2 * matrices.size, transcendentals=0
        ),
        name="project",
    )(pattern, counts, exponents, values, matrices)


def finish_kernel(share, weights, far, below, above, own, keep, send):
    parity = lax.rem(lax.axis_index("dom"), 2)
    columns = own.shape[1]
    tile = max(columns, 2 * share)
    for first in range(0, own.shape[0], tile):
        rows = slice(first, first + tile)
        total = own[rows, :]
        start = 0
        for blocks in (far, below, above):
            stop = start + blocks.shape[0]
            total += jnp.dot(weights[rows, start:stop], blocks[...], preferred_element_type=jnp.float32)
            start = stop
        halves = total.reshape(-1, 2, share, columns)
        even = halves[:, 0].reshape(-1, columns)
        odd = halves[:, 1].reshape(-1, columns)
        half = slice(first // 2, (first + tile) // 2)
        keep[half, :] = jnp.where(parity == 0, even, odd)
        send[half, :] = jnp.where(parity == 0, odd, even)


def finish(weights, far, below, above, own, share):
    half = jax.ShapeDtypeStruct((own.shape[0] // 2, own.shape[1]), jnp.float32)
    return pl.pallas_call(
        functools.partial(finish_kernel, share),
        out_shape=(half, half),
        in_specs=[VMEM] * 5,
        out_specs=(VMEM, VMEM),
        compiler_params=pltpu.CompilerParams(vmem_limit_bytes=24 * 2**20),
        name="finish",
    )(weights, far, below, above, own)


def on_device(matrices, values, exponents, pattern, block_counts, send_lists, ghost_counts):
    parts = lax.axis_size("dom")
    terms = pattern.shape[0]
    size = matrices.shape[-1]
    lent = send_lists.shape[2]
    row_count, columns = values.shape

    far, after, before = pack(jnp.transpose(send_lists, (0, 2, 1)), exponents, values, size)
    far = lax.all_to_all(far, "dom", split_axis=0, concat_axis=0, tiled=True)
    below = lax.ppermute(after, "dom", [(p, p + 1) for p in range(parts - 1)])
    above = lax.ppermute(before, "dom", [(p + 1, p) for p in range(parts - 1)])

    weights, own = project(
        jnp.transpose(pattern, (2, 0, 1)), block_counts, exponents, values, matrices, parts, lent
    )
    share = terms * columns // parts
    flat = lambda a: a.reshape(-1, columns)
    keep, send = finish(weights, flat(far), flat(below), flat(above), own, share)
    both = keep + lax.ppermute(send, "dom", [(p, p ^ 1) for p in range(parts)])
    both = both.astype(jnp.bfloat16).reshape(parts // 2, share, columns)
    groups = [list(range(core, parts, 2)) for core in range(2)]
    pieces = lax.all_to_all(both, "dom", split_axis=0, concat_axis=0, tiled=True, axis_index_groups=groups)
    summed = jnp.sum(pieces.astype(jnp.float32), axis=0)
    return summed * (1.0 / math.sqrt(row_count * parts))


def solution(mesh):
    return jax.shard_map(
        on_device,
        mesh=mesh,
        in_specs=(
            P(None, ("group", "dom"), None, None, None),
            P(("group", "dom"), None),
            P(("group", "dom")),
            P(None, ("group", "dom"), None),
            P(None, ("group", "dom")),
            P(("group", "dom"), None, None),
            P(("group", "dom"), None),
        ),
        out_specs=P(("group", "dom"), None),
        check_vma=False,
    )
```

```python
import functools
import math

import jax
import jax.numpy as jnp
from jax import lax
from jax.experimental import pallas as pl
from jax.experimental.pallas import tpu as pltpu
from jax.sharding import PartitionSpec as P

SMEM = pl.BlockSpec(memory_space=pltpu.SMEM)
VMEM = pl.BlockSpec(memory_space=pltpu.VMEM)
ANY = pl.BlockSpec(memory_space=pl.ANY)


def power_of_two(exponent):
    return (lax.shift_left(jnp.int32(1), exponent + 2).astype(jnp.float32) * 0.25).astype(jnp.bfloat16)


def pack_kernel(parts, size, lists, exponents, values, far, after, before):
    me = lax.axis_index("dom")
    lent = lists.shape[1]
    upper = jnp.minimum(me + 1, parts - 1)
    lower = jnp.maximum(me - 1, 0)

    def lend(block, out, n):
        rows = pl.ds(pl.multiple_of(block * size, size), size)
        out[n] = values[rows, :] * power_of_two(exponents[block])

    for p in range(parts):
        lend(lists[0, 0, p], far, p)
    for g in range(1, lent):
        lend(lists[0, g, upper], after, g - 1)
        lend(lists[0, g, lower], before, g - 1)


def pack(lists, exponents, values, size):
    lent, parts = lists.shape[1:]
    columns = values.shape[1]
    block = lambda n: jax.ShapeDtypeStruct((n, size, columns), values.dtype)
    return pl.pallas_call(
        functools.partial(pack_kernel, parts, size),
        out_shape=(block(parts), block(lent - 1), block(lent - 1)),
        in_specs=[SMEM, SMEM, VMEM],
        out_specs=(VMEM, VMEM, VMEM),
        name="pack",
    )(lists, exponents, values)


def project_kernel(parts, lent, middle, wide, pattern_in, counts_in, exponents_in, values_in, matrices, *refs):
    kept, terms, owned = pattern_in.shape
    weights, partial = refs[:2]
    (acc, basis, turned, split, held, staged, values, pattern, counts, own_table, ghost_table,
     own_slots, ghost_slots, exponents, listed, came, read, moved, went) = refs[2:]
    me = lax.axis_index("dom")
    size = held.shape[-1]
    columns = values.shape[1]
    ghosts = parts + 2 * (lent - 1)
    trash = terms * ghosts
    steps = owned // 2

    def fetch(step):
        pair = pl.ds(2 * step, 2)
        return pltpu.make_async_copy(matrices.at[:, pair], held.at[:, pair], came.at[step])

    reads = [
        pltpu.make_async_copy(source, target, read.at[n])
        for n, (source, target) in enumerate(
            [(pattern_in, pattern), (counts_in, counts), (exponents_in, exponents), (values_in, values)]
        )
    ]
    for copy in reads:
        copy.start()
    for step in range(2):
        fetch(step).start()

    def clear(n, carry):
        acc[n] = jnp.zeros(acc.shape[1:], acc.dtype)
        return carry

    lax.fori_loop(0, acc.shape[0], clear, 0)
    basis[owned] = jnp.zeros(basis.shape[1:], basis.dtype)
    partial[...] = jnp.zeros(partial.shape, partial.dtype)
    reads[0].wait()
    reads[1].wait()

    slot = pattern[...]
    k, q, b = (lax.broadcasted_iota(jnp.int32, slot.shape, n) for n in range(3))
    present = k < counts[...][None]
    ghost = present & (slot >= owned)
    lender, which = (slot - owned) // lent, (slot - owned) % lent
    further = parts + which - 1 + jnp.where(lender > me, lent - 1, 0)
    target = q * ghosts + jnp.where(which == 0, lender, further)
    some = jnp.max(ghost.astype(jnp.int32), axis=0, keepdims=True)
    own_table[...] = jnp.where(present & (slot < owned), slot, owned) + jnp.where(k == 0, 256 * some, 0)
    ghost_table[...] = jnp.where(ghost, (1 << 30) + (target << 16) + (b << 8) + (q << 4) + k, 0)
    moves = [
        pltpu.make_async_copy(own_table, own_slots, moved.at[0]),
        pltpu.make_async_copy(ghost_table, ghost_slots, moved.at[1]),
    ]
    for copy in moves:
        copy.start()
    for step in range(2, steps):
        fetch(step).start()
    for copy in moves + reads[2:]:
        copy.wait()

    def prepare(n, found):
        rows = pl.ds(pl.multiple_of(n * size, size), size)
        scaled = values[rows, :] * power_of_two(exponents[n])
        basis[n] = scaled
        turned[n] = scaled.T
        for q in range(terms):
            for k in range(kept):
                word = ghost_slots[k, q, n]
                listed[found] = word
                found += lax.shift_right_logical(word, 30)
        return found

    found = lax.fori_loop(0, owned, prepare, jnp.int32(0))
    for n in range(2 * wide):
        listed[found + n] = trash << 16

    def multiply(step):
        slot = lax.rem(step, 2)
        for sub in range(2):
            b = 2 * step + sub
            for q in range(terms):
                words = [own_slots[k, q, b] for k in range(kept)]
                mixed = lax.shift_right_logical(words[0], 8)
                words[0] = words[0] & 255
                left = jnp.concatenate([held[q, b, k] for k in range(kept)], axis=1)
                table = jnp.concatenate([basis[word] for word in words], axis=0)
                exact = jnp.dot(left, table, preferred_element_type=jnp.float32)
                upper = exact.astype(jnp.bfloat16)
                rest = (exact - upper.astype(jnp.float32)) * mixed.astype(jnp.float32)
                split[slot, q, sub * size:(sub + 1) * size, :] = upper
                split[slot, q, (2 + sub) * size:(3 + sub) * size, :] = rest.astype(jnp.bfloat16)

    def gather(step):
        slot = lax.rem(step, 2)
        left = jnp.concatenate([turned[2 * step], turned[2 * step + 1]] * 2, axis=1)
        for q in range(terms):
            rows = slice(q * columns, (q + 1) * columns)
            partial[rows, :] += jnp.dot(left, split[slot, q], preferred_element_type=jnp.float32)

    def body(step, carry):
        gather(step - 1)
        multiply(step)
        return carry

    def first_body(step, carry):
        fetch(step).wait()
        return body(step, carry)

    fetch(0).wait()
    multiply(jnp.int32(0))
    lax.fori_loop(1, middle, first_body, 0)
    for step in range(middle, steps):
        fetch(step).wait()
    nothing = jnp.zeros((size, size), jnp.bfloat16)

    def take(n):
        word = listed[n]
        field = lambda place, bits: lax.shift_right_logical(word, place) & ((1 << bits) - 1)
        b = field(8, 8)
        return turned[b], held[field(4, 4), b, field(0, 4)], field(16, 14)

    def project_ghosts(n, carry):
        for m in range(wide):
            left_a, block_a, target_a = take(n * 2 * wide + 2 * m)
            left_b, block_b, target_b = take(n * 2 * wide + 2 * m + 1)
            left = jnp.concatenate([left_a, left_b], axis=1)
            right = jnp.concatenate([
                jnp.concatenate([block_a, nothing], axis=1),
                jnp.concatenate([nothing, block_b], axis=1),
            ], axis=0)
            both = jnp.dot(left, right, preferred_element_type=jnp.float32)
            acc[target_a] += both[:, :size]
            acc[target_b] += both[:, size:]
        return carry

    lax.fori_loop(0, lax.div(found + 2 * wide - 1, 2 * wide), project_ghosts, 0)

    leaving = []
    for q in range(terms):
        for g in range(ghosts):
            staged[q, :, g * size:(g + 1) * size] = acc[q * ghosts + g].astype(jnp.bfloat16)
        leaving.append(pltpu.make_async_copy(staged.at[q], weights.at[q], went.at[q]))
        leaving[-1].start()
    lax.fori_loop(middle, steps, body, 0)
    gather(steps - 1)
    for copy in leaving:
        copy.wait()


def project(pattern, counts, exponents, values, matrices, parts, lent):
    kept, terms, owned = pattern.shape
    size = matrices.shape[-1]
    columns = values.shape[1]
    ghosts = parts + 2 * (lent - 1)
    weights = jax.ShapeDtypeStruct((terms, columns, ghosts * size), jnp.bfloat16)
    partial = jax.ShapeDtypeStruct((terms * columns, columns), jnp.float32)
    wide = 8
    return pl.pallas_call(
        functools.partial(project_kernel, parts, lent, owned // 3, wide),
        out_shape=(weights, partial),
        in_specs=[ANY] * 5,
        out_specs=(ANY, VMEM),
        scratch_shapes=[
            pltpu.VMEM((terms * ghosts + 1, columns, size), jnp.float32),
            pltpu.VMEM((owned + 1, size, columns), jnp.bfloat16),
            pltpu.VMEM((owned, columns, size), jnp.bfloat16),
            pltpu.VMEM((2, terms, 4 * size, columns), jnp.bfloat16),
            pltpu.VMEM(matrices.shape, jnp.bfloat16),
            pltpu.VMEM(weights.shape, weights.dtype),
            pltpu.VMEM(values.shape, values.dtype),
            pltpu.VMEM(pattern.shape, jnp.int32),
            pltpu.VMEM(counts.shape, jnp.int32),
            pltpu.VMEM(pattern.shape, jnp.int32),
            pltpu.VMEM(pattern.shape, jnp.int32),
            pltpu.SMEM(pattern.shape, jnp.int32),
            pltpu.SMEM(pattern.shape, jnp.int32),
            pltpu.SMEM(exponents.shape, jnp.int32),
            pltpu.SMEM((owned * terms * kept + 2 * wide,), jnp.int32),
            pltpu.SemaphoreType.DMA((owned // 2,)),
            pltpu.SemaphoreType.DMA((4,)),
            pltpu.SemaphoreType.DMA((2,)),
            pltpu.SemaphoreType.DMA((terms,)),
        ],
        compiler_params=pltpu.CompilerParams(vmem_limit_bytes=60 * 2**20),
        cost_estimate=pl.CostEstimate(
            flops=2 * matrices.size * columns, bytes_accessed=2 * matrices.size, transcendentals=0
        ),
        name="project",
    )(pattern, counts, exponents, values, matrices)


def finish_kernel(share, weights, far, below, above, own, keep, send):
    parity = lax.rem(lax.axis_index("dom"), 2)
    columns = own.shape[1]
    tile = max(columns, 2 * share)
    for first in range(0, own.shape[0], tile):
        rows = slice(first, first + tile)
        total = own[rows, :]
        start = 0
        for blocks in (far, below, above):
            stop = start + blocks.shape[0]
            total += jnp.dot(weights[rows, start:stop], blocks[...], preferred_element_type=jnp.float32)
            start = stop
        halves = total.reshape(-1, 2, share, columns)
        even = halves[:, 0].reshape(-1, columns)
        odd = halves[:, 1].reshape(-1, columns)
        half = slice(first // 2, (first + tile) // 2)
        keep[half, :] = jnp.where(parity == 0, even, odd)
        send[half, :] = jnp.where(parity == 0, odd, even)


def finish(weights, far, below, above, own, share):
    half = jax.ShapeDtypeStruct((own.shape[0] // 2, own.shape[1]), jnp.float32)
    return pl.pallas_call(
        functools.partial(finish_kernel, share),
        out_shape=(half, half),
        in_specs=[VMEM] * 5,
        out_specs=(VMEM, VMEM),
        compiler_params=pltpu.CompilerParams(vmem_limit_bytes=4 * 2**20),
        name="finish",
    )(weights, far, below, above, own)


def on_device(matrices, values, exponents, pattern, block_counts, send_lists, ghost_counts):
    parts = lax.axis_size("dom")
    terms = pattern.shape[0]
    size = matrices.shape[-1]
    lent = send_lists.shape[2]
    row_count, columns = values.shape

    far, after, before = pack(jnp.transpose(send_lists, (0, 2, 1)), exponents, values, size)
    far = lax.all_to_all(far, "dom", split_axis=0, concat_axis=0, tiled=True)
    below = lax.ppermute(after, "dom", [(p, p + 1) for p in range(parts - 1)])
    above = lax.ppermute(before, "dom", [(p + 1, p) for p in range(parts - 1)])

    weights, own = project(
        jnp.transpose(pattern, (2, 0, 1)), block_counts, exponents, values, matrices, parts, lent
    )
    share = terms * columns // parts
    flat = lambda a: a.reshape(-1, columns)
    keep, send = finish(weights.reshape(terms * columns, -1), flat(far), flat(below), flat(above), own, share)
    both = keep + lax.ppermute(send, "dom", [(p, p ^ 1) for p in range(parts)])
    both = both.astype(jnp.bfloat16).reshape(parts // 2, share, columns)
    groups = [list(range(core, parts, 2)) for core in range(2)]
    pieces = lax.all_to_all(both, "dom", split_axis=0, concat_axis=0, tiled=True, axis_index_groups=groups)
    summed = jnp.sum(pieces.astype(jnp.float32), axis=0)
    return summed * (1.0 / math.sqrt(row_count * parts))


def solution(mesh):
    return jax.shard_map(
        on_device,
        mesh=mesh,
        in_specs=(
            P(None, ("group", "dom"), None, None, None),
            P(("group", "dom"), None),
            P(("group", "dom")),
            P(None, ("group", "dom"), None),
            P(None, ("group", "dom")),
            P(("group", "dom"), None, None),
            P(("group", "dom"), None),
        ),
        out_specs=P(("group", "dom"), None),
        check_vma=False,
    )
```

```python
import functools
import math

import jax
import jax.numpy as jnp
from jax import lax
from jax.experimental import pallas as pl
from jax.experimental.pallas import tpu as pltpu
from jax.sharding import PartitionSpec as P

SMEM = pl.BlockSpec(memory_space=pltpu.SMEM)
VMEM = pl.BlockSpec(memory_space=pltpu.VMEM)
ANY = pl.BlockSpec(memory_space=pl.ANY)


def power_of_two(exponent):
    return (lax.shift_left(jnp.int32(1), exponent + 2).astype(jnp.float32) * 0.25).astype(jnp.bfloat16)


def pack_kernel(parts, size, lists, exponents, values, far, after, before):
    me = lax.axis_index("dom")
    lent = lists.shape[1]
    upper = jnp.minimum(me + 1, parts - 1)
    lower = jnp.maximum(me - 1, 0)

    def lend(block, out, n):
        rows = pl.ds(pl.multiple_of(block * size, size), size)
        out[n] = values[rows, :] * power_of_two(exponents[block])

    for p in range(parts):
        lend(lists[0, 0, p], far, p)
    for g in range(1, lent):
        lend(lists[0, g, upper], after, g - 1)
        lend(lists[0, g, lower], before, g - 1)


def pack(lists, exponents, values, size):
    lent, parts = lists.shape[1:]
    columns = values.shape[1]
    block = lambda n: jax.ShapeDtypeStruct((n, size, columns), values.dtype)
    return pl.pallas_call(
        functools.partial(pack_kernel, parts, size),
        out_shape=(block(parts), block(lent - 1), block(lent - 1)),
        in_specs=[SMEM, SMEM, VMEM],
        out_specs=(VMEM, VMEM, VMEM),
        name="pack",
    )(lists, exponents, values)


def project_kernel(parts, lent, middle, wide, share, pattern_in, counts_in, exponents_in, values_in, matrices, *refs):
    kept, terms, owned = pattern_in.shape
    outs = refs[:2]
    (acc, basis, turned, split, held, staged, partial, values, pattern, counts,
     own_table, ghost_table, own_slots, ghost_slots, exponents, listed, came, read, moved, went) = refs[2:]
    me = lax.axis_index("dom")
    size = held.shape[-1]
    columns = values.shape[1]
    ghosts = parts + 2 * (lent - 1)
    trash = terms * ghosts
    steps = owned // 2

    def fetch(step):
        pair = pl.ds(2 * step, 2)
        return pltpu.make_async_copy(matrices.at[:, pair], held.at[:, pair], came.at[step])

    reads = [
        pltpu.make_async_copy(source, target, read.at[n])
        for n, (source, target) in enumerate(
            [(pattern_in, pattern), (counts_in, counts), (exponents_in, exponents), (values_in, values)]
        )
    ]
    for copy in reads:
        copy.start()
    for step in range(2):
        fetch(step).start()

    def clear(n, carry):
        acc[n] = jnp.zeros(acc.shape[1:], acc.dtype)
        return carry

    lax.fori_loop(0, acc.shape[0], clear, 0)
    basis[owned] = jnp.zeros(basis.shape[1:], basis.dtype)
    partial[...] = jnp.zeros(partial.shape, partial.dtype)
    reads[0].wait()
    reads[1].wait()

    slot = pattern[...]
    k, q, b = (lax.broadcasted_iota(jnp.int32, slot.shape, n) for n in range(3))
    present = k < counts[...][None]
    ghost = present & (slot >= owned)
    lender, which = (slot - owned) // lent, (slot - owned) % lent
    further = parts + which - 1 + jnp.where(lender > me, lent - 1, 0)
    target = q * ghosts + jnp.where(which == 0, lender, further)
    some = jnp.max(ghost.astype(jnp.int32), axis=0, keepdims=True)
    own_table[...] = jnp.where(present & (slot < owned), slot, owned) + jnp.where(k == 0, 256 * some, 0)
    ghost_table[...] = jnp.where(ghost, (1 << 30) + (target << 16) + (b << 8) + (q << 4) + k, 0)
    moves = [
        pltpu.make_async_copy(own_table, own_slots, moved.at[0]),
        pltpu.make_async_copy(ghost_table, ghost_slots, moved.at[1]),
    ]
    for copy in moves:
        copy.start()
    for step in range(2, steps):
        fetch(step).start()
    for copy in moves + reads[2:]:
        copy.wait()

    def prepare(n, found):
        rows = pl.ds(pl.multiple_of(n * size, size), size)
        scaled = values[rows, :] * power_of_two(exponents[n])
        basis[n] = scaled
        turned[n] = scaled.T
        for q in range(terms):
            for k in range(kept):
                word = ghost_slots[k, q, n]
                listed[found] = word
                found += lax.shift_right_logical(word, 30)
        return found

    found = lax.fori_loop(0, owned, prepare, jnp.int32(0))
    for n in range(2 * wide):
        listed[found + n] = trash << 16

    def multiply(step):
        slot = lax.rem(step, 2)
        for sub in range(2):
            b = 2 * step + sub
            for q in range(terms):
                words = [own_slots[k, q, b] for k in range(kept)]
                mixed = lax.shift_right_logical(words[0], 8)
                words[0] = words[0] & 255
                left = jnp.concatenate([held[q, b, k] for k in range(kept)], axis=1)
                table = jnp.concatenate([basis[word] for word in words], axis=0)
                exact = jnp.dot(left, table, preferred_element_type=jnp.float32)
                upper = exact.astype(jnp.bfloat16)
                rest = (exact - upper.astype(jnp.float32)) * mixed.astype(jnp.float32)
                split[slot, q, sub * size:(sub + 1) * size, :] = upper
                split[slot, q, (2 + sub) * size:(3 + sub) * size, :] = rest.astype(jnp.bfloat16)

    def gather(step):
        slot = lax.rem(step, 2)
        left = jnp.concatenate([turned[2 * step], turned[2 * step + 1]] * 2, axis=1)
        for q in range(terms):
            rows = slice(q * columns, (q + 1) * columns)
            partial[rows, :] += jnp.dot(left, split[slot, q], preferred_element_type=jnp.float32)

    def body(step, carry):
        gather(step - 1)
        multiply(step)
        return carry

    def first_body(step, carry):
        fetch(step).wait()
        return body(step, carry)

    fetch(0).wait()
    multiply(jnp.int32(0))
    lax.fori_loop(1, middle, first_body, 0)
    for step in range(middle, steps):
        fetch(step).wait()
    nothing = jnp.zeros((size, size), jnp.bfloat16)

    def take(n):
        word = listed[n]
        field = lambda place, bits: lax.shift_right_logical(word, place) & ((1 << bits) - 1)
        b = field(8, 8)
        return turned[b], held[field(4, 4), b, field(0, 4)], field(16, 14)

    def project_ghosts(n, carry):
        for m in range(wide):
            left_a, block_a, target_a = take(n * 2 * wide + 2 * m)
            left_b, block_b, target_b = take(n * 2 * wide + 2 * m + 1)
            left = jnp.concatenate([left_a, left_b], axis=1)
            right = jnp.concatenate([
                jnp.concatenate([block_a, nothing], axis=1),
                jnp.concatenate([nothing, block_b], axis=1),
            ], axis=0)
            both = jnp.dot(left, right, preferred_element_type=jnp.float32)
            acc[target_a] += both[:, :size]
            acc[target_b] += both[:, size:]
        return carry

    lax.fori_loop(0, lax.div(found + 2 * wide - 1, 2 * wide), project_ghosts, 0)

    parity = lax.rem(me, 2)
    runs = columns // (2 * share)

    def run(m, side):
        return pl.ds(pl.multiple_of((2 * m + side) * share, share), share)

    deep = ghosts * size
    leaving = []

    def leave(n, lanes):
        leaving.append(pltpu.make_async_copy(staged.at[n, :, lanes], outs[n].at[:, lanes], went.at[len(leaving)]))
        leaving[-1].start()

    sides = (1 - parity, parity)
    for n, side in enumerate(sides):
        for q in range(terms):
            for m in range(runs):
                rows = pl.ds((q * runs + m) * share, share)
                for g in range(ghosts):
                    lanes = slice(g * size, (g + 1) * size)
                    staged[n, rows, lanes] = acc[q * ghosts + g, run(m, side), :].astype(jnp.bfloat16)
        leave(n, slice(0, deep))
    lax.fori_loop(middle, steps, body, 0)
    gather(steps - 1)
    for n, side in enumerate(sides):
        for q in range(terms):
            for m in range(runs):
                exact = partial[pl.ds(pl.multiple_of(q * columns + (2 * m + side) * share, share), share), :]
                upper = exact.astype(jnp.bfloat16)
                rows = pl.ds((q * runs + m) * share, share)
                staged[n, rows, deep:deep + columns] = upper
                staged[n, rows, deep + columns:] = (exact - upper.astype(jnp.float32)).astype(jnp.bfloat16)
        leave(n, slice(deep, deep + 2 * columns))
    for copy in leaving:
        copy.wait()


def project(pattern, counts, exponents, values, matrices, parts, lent):
    kept, terms, owned = pattern.shape
    size = matrices.shape[-1]
    columns = values.shape[1]
    ghosts = parts + 2 * (lent - 1)
    half = jax.ShapeDtypeStruct((terms * columns // 2, ghosts * size + 2 * columns), jnp.bfloat16)
    wide = 8
    return pl.pallas_call(
        functools.partial(project_kernel, parts, lent, owned // 3, wide, terms * columns // parts),
        out_shape=(half, half),
        in_specs=[ANY] * 5,
        out_specs=(ANY, ANY),
        scratch_shapes=[
            pltpu.VMEM((terms * ghosts + 1, columns, size), jnp.float32),
            pltpu.VMEM((owned + 1, size, columns), jnp.bfloat16),
            pltpu.VMEM((owned, columns, size), jnp.bfloat16),
            pltpu.VMEM((2, terms, 4 * size, columns), jnp.bfloat16),
            pltpu.VMEM(matrices.shape, jnp.bfloat16),
            pltpu.VMEM((2,) + half.shape, half.dtype),
            pltpu.VMEM((terms * columns, columns), jnp.float32),
            pltpu.VMEM(values.shape, values.dtype),
            pltpu.VMEM(pattern.shape, jnp.int32),
            pltpu.VMEM(counts.shape, jnp.int32),
            pltpu.VMEM(pattern.shape, jnp.int32),
            pltpu.VMEM(pattern.shape, jnp.int32),
            pltpu.SMEM(pattern.shape, jnp.int32),
            pltpu.SMEM(pattern.shape, jnp.int32),
            pltpu.SMEM(exponents.shape, jnp.int32),
            pltpu.SMEM((owned * terms * kept + 2 * wide,), jnp.int32),
            pltpu.SemaphoreType.DMA((owned // 2,)),
            pltpu.SemaphoreType.DMA((4,)),
            pltpu.SemaphoreType.DMA((2,)),
            pltpu.SemaphoreType.DMA((4,)),
        ],
        compiler_params=pltpu.CompilerParams(vmem_limit_bytes=60 * 2**20),
        cost_estimate=pl.CostEstimate(
            flops=2 * matrices.size * columns, bytes_accessed=2 * matrices.size, transcendentals=0
        ),
        name="project",
    )(pattern, counts, exponents, values, matrices)


def half_kernel(weights, far, below, above, out):
    columns = out.shape[1]
    deep = weights.shape[1] - 2 * columns
    total = weights[:, deep:deep + columns].astype(jnp.float32) + weights[:, deep + columns:].astype(jnp.float32)
    start = 0
    for block in (far, below, above):
        stop = start + block.shape[0]
        total += jnp.dot(weights[:, start:stop], block[...], preferred_element_type=jnp.float32)
        start = stop
    out[...] = total


def half_partial(weights, far, below, above):
    rows, columns = weights.shape[0], far.shape[1]
    return pl.pallas_call(
        half_kernel,
        out_shape=jax.ShapeDtypeStruct((rows, columns), jnp.float32),
        in_specs=[VMEM] * 4,
        out_specs=VMEM,
        compiler_params=pltpu.CompilerParams(vmem_limit_bytes=4 * 2**20),
        cost_estimate=pl.CostEstimate(
            flops=2 * weights.size * columns, bytes_accessed=2 * weights.size, transcendentals=0
        ),
        name="half_partial",
    )(weights, far, below, above)


def on_device(matrices, values, exponents, pattern, block_counts, send_lists, ghost_counts):
    parts = lax.axis_size("dom")
    terms = pattern.shape[0]
    size = matrices.shape[-1]
    lent = send_lists.shape[2]
    row_count, columns = values.shape

    far, after, before = pack(jnp.transpose(send_lists, (0, 2, 1)), exponents, values, size)
    far = lax.all_to_all(far, "dom", split_axis=0, concat_axis=0, tiled=True)
    below = lax.ppermute(after, "dom", [(p, p + 1) for p in range(parts - 1)])
    above = lax.ppermute(before, "dom", [(p + 1, p) for p in range(parts - 1)])

    send_weights, keep_weights = project(
        jnp.transpose(pattern, (2, 0, 1)), block_counts, exponents, values, matrices, parts, lent
    )
    flat = lambda a: a.reshape(-1, columns)
    ghosts = (flat(far), flat(below), flat(above))
    send = half_partial(send_weights, *ghosts)
    came = lax.ppermute(send, "dom", [(p, p ^ 1) for p in range(parts)])
    both = came + half_partial(keep_weights, *ghosts)
    share = terms * columns // parts
    both = both.astype(jnp.bfloat16).reshape(parts // 2, share, columns)
    groups = [list(range(core, parts, 2)) for core in range(2)]
    pieces = lax.all_to_all(both, "dom", split_axis=0, concat_axis=0, tiled=True, axis_index_groups=groups)
    summed = jnp.sum(pieces.astype(jnp.float32), axis=0)
    return summed * (1.0 / math.sqrt(row_count * parts))


def solution(mesh):
    return jax.shard_map(
        on_device,
        mesh=mesh,
        in_specs=(
            P(None, ("group", "dom"), None, None, None),
            P(("group", "dom"), None),
            P(("group", "dom")),
            P(None, ("group", "dom"), None),
            P(None, ("group", "dom")),
            P(("group", "dom"), None, None),
            P(("group", "dom"), None),
        ),
        out_specs=P(("group", "dom"), None),
        check_vma=False,
    )
```

```python
import functools
import math

import jax
import jax.numpy as jnp
from jax import lax
from jax.experimental import pallas as pl
from jax.experimental.pallas import tpu as pltpu
from jax.sharding import PartitionSpec as P

SMEM = pl.BlockSpec(memory_space=pltpu.SMEM)
VMEM = pl.BlockSpec(memory_space=pltpu.VMEM)
ANY = pl.BlockSpec(memory_space=pl.ANY)


def power_of_two(exponent):
    return (lax.shift_left(jnp.int32(1), exponent + 2).astype(jnp.float32) * 0.25).astype(jnp.bfloat16)


def neighbours(me, parts):
    parity = lax.rem(me, 2)
    return me + 1 - 2 * parity, jnp.clip(me - 1 + 2 * parity, 0, parts - 1)


def pack_kernel(parts, size, lists, exponents, values, far, inner, outer):
    me = lax.axis_index("dom")
    lent = lists.shape[1]
    mate, other = neighbours(me, parts)

    def lend(block, out, n):
        rows = pl.ds(pl.multiple_of(block * size, size), size)
        out[n] = values[rows, :] * power_of_two(exponents[block])

    for p in range(parts):
        lend(lists[0, 0, p], far, p)
    for g in range(1, lent):
        lend(lists[0, g, mate], inner, g - 1)
        lend(lists[0, g, other], outer, g - 1)


def pack(lists, exponents, values, size):
    lent, parts = lists.shape[1:]
    columns = values.shape[1]
    block = lambda n: jax.ShapeDtypeStruct((n, size, columns), values.dtype)
    return pl.pallas_call(
        functools.partial(pack_kernel, parts, size),
        out_shape=(block(parts), block(lent - 1), block(lent - 1)),
        in_specs=[SMEM, SMEM, VMEM],
        out_specs=(VMEM, VMEM, VMEM),
        name="pack",
    )(lists, exponents, values)


def project_kernel(parts, lent, middle, wide, share, pattern_in, counts_in, exponents_in, values_in, matrices, *refs):
    kept, terms, owned = pattern_in.shape
    outs = refs[:2]
    (acc, basis, turned, split, held, staged, partial, values, pattern, counts,
     own_table, ghost_table, own_slots, ghost_slots, exponents, listed, came, read, moved, went) = refs[2:]
    me = lax.axis_index("dom")
    size = held.shape[-1]
    columns = values.shape[1]
    mate, _ = neighbours(me, parts)
    ghosts = parts + 2 * (lent - 1)
    trash = terms * ghosts
    steps = owned // 2

    def fetch(step):
        pair = pl.ds(2 * step, 2)
        return pltpu.make_async_copy(matrices.at[:, pair], held.at[:, pair], came.at[step])

    reads = [
        pltpu.make_async_copy(source, target, read.at[n])
        for n, (source, target) in enumerate(
            [(pattern_in, pattern), (counts_in, counts), (exponents_in, exponents), (values_in, values)]
        )
    ]
    for copy in reads:
        copy.start()
    for step in range(2):
        fetch(step).start()

    def clear(n, carry):
        acc[n] = jnp.zeros(acc.shape[1:], acc.dtype)
        return carry

    lax.fori_loop(0, acc.shape[0], clear, 0)
    basis[owned] = jnp.zeros(basis.shape[1:], basis.dtype)
    partial[...] = jnp.zeros(partial.shape, partial.dtype)
    reads[0].wait()
    reads[1].wait()

    slot = pattern[...]
    k, q, b = (lax.broadcasted_iota(jnp.int32, slot.shape, n) for n in range(3))
    present = k < counts[...][None]
    ghost = present & (slot >= owned)
    lender, which = (slot - owned) // lent, (slot - owned) % lent
    further = parts + which - 1 + jnp.where(lender == mate, 0, lent - 1)
    target = q * ghosts + jnp.where(which == 0, lender, further)
    some = jnp.max(ghost.astype(jnp.int32), axis=0, keepdims=True)
    own_table[...] = jnp.where(present & (slot < owned), slot, owned) + jnp.where(k == 0, 256 * some, 0)
    ghost_table[...] = jnp.where(ghost, (1 << 30) + (target << 16) + (b << 8) + (q << 4) + k, 0)
    moves = [
        pltpu.make_async_copy(own_table, own_slots, moved.at[0]),
        pltpu.make_async_copy(ghost_table, ghost_slots, moved.at[1]),
    ]
    for copy in moves:
        copy.start()
    for step in range(2, steps):
        fetch(step).start()
    for copy in moves + reads[2:]:
        copy.wait()

    def prepare(n, found):
        rows = pl.ds(pl.multiple_of(n * size, size), size)
        scaled = values[rows, :] * power_of_two(exponents[n])
        basis[n] = scaled
        turned[n] = scaled.T
        for q in range(terms):
            for k in range(kept):
                word = ghost_slots[k, q, n]
                listed[found] = word
                found += lax.shift_right_logical(word, 30)
        return found

    found = lax.fori_loop(0, owned, prepare, jnp.int32(0))
    for n in range(2 * wide):
        listed[found + n] = trash << 16

    def multiply(step):
        slot = lax.rem(step, 2)
        for sub in range(2):
            b = 2 * step + sub
            for q in range(terms):
                words = [own_slots[k, q, b] for k in range(kept)]
                mixed = lax.shift_right_logical(words[0], 8)
                words[0] = words[0] & 255
                left = jnp.concatenate([held[q, b, k] for k in range(kept)], axis=1)
                table = jnp.concatenate([basis[word] for word in words], axis=0)
                exact = jnp.dot(left, table, preferred_element_type=jnp.float32)
                upper = exact.astype(jnp.bfloat16)
                rest = (exact - upper.astype(jnp.float32)) * mixed.astype(jnp.float32)
                split[slot, q, sub * size:(sub + 1) * size, :] = upper
                split[slot, q, (2 + sub) * size:(3 + sub) * size, :] = rest.astype(jnp.bfloat16)

    def gather(step):
        slot = lax.rem(step, 2)
        left = jnp.concatenate([turned[2 * step], turned[2 * step + 1]] * 2, axis=1)
        for q in range(terms):
            rows = slice(q * columns, (q + 1) * columns)
            partial[rows, :] += jnp.dot(left, split[slot, q], preferred_element_type=jnp.float32)

    def body(step, carry):
        gather(step - 1)
        multiply(step)
        return carry

    def first_body(step, carry):
        fetch(step).wait()
        return body(step, carry)

    fetch(0).wait()
    multiply(jnp.int32(0))
    lax.fori_loop(1, middle, first_body, 0)
    for step in range(middle, steps):
        fetch(step).wait()
    nothing = jnp.zeros((size, size), jnp.bfloat16)

    def take(n):
        word = listed[n]
        field = lambda place, bits: lax.shift_right_logical(word, place) & ((1 << bits) - 1)
        b = field(8, 8)
        return turned[b], held[field(4, 4), b, field(0, 4)], field(16, 14)

    def project_ghosts(n, carry):
        for m in range(wide):
            left_a, block_a, target_a = take(n * 2 * wide + 2 * m)
            left_b, block_b, target_b = take(n * 2 * wide + 2 * m + 1)
            left = jnp.concatenate([left_a, left_b], axis=1)
            right = jnp.concatenate([
                jnp.concatenate([block_a, nothing], axis=1),
                jnp.concatenate([nothing, block_b], axis=1),
            ], axis=0)
            both = jnp.dot(left, right, preferred_element_type=jnp.float32)
            acc[target_a] += both[:, :size]
            acc[target_b] += both[:, size:]
        return carry

    lax.fori_loop(0, lax.div(found + 2 * wide - 1, 2 * wide), project_ghosts, 0)

    parity = lax.rem(me, 2)
    runs = columns // (2 * share)

    def run(m, side):
        return pl.ds(pl.multiple_of((2 * m + side) * share, share), share)

    deep = ghosts * size
    leaving = []

    def leave(n, lanes):
        leaving.append(pltpu.make_async_copy(staged.at[n, :, lanes], outs[n].at[:, lanes], went.at[len(leaving)]))
        leaving[-1].start()

    sides = (1 - parity, parity)
    for n, side in enumerate(sides):
        for q in range(terms):
            for m in range(runs):
                rows = pl.ds((q * runs + m) * share, share)
                for g in range(ghosts):
                    lanes = slice(g * size, (g + 1) * size)
                    staged[n, rows, lanes] = acc[q * ghosts + g, run(m, side), :].astype(jnp.bfloat16)
        leave(n, slice(0, deep))
    lax.fori_loop(middle, steps, body, 0)
    gather(steps - 1)
    for n, side in enumerate(sides):
        for q in range(terms):
            for m in range(runs):
                exact = partial[pl.ds(pl.multiple_of(q * columns + (2 * m + side) * share, share), share), :]
                upper = exact.astype(jnp.bfloat16)
                rows = pl.ds((q * runs + m) * share, share)
                staged[n, rows, deep:deep + columns] = upper
                staged[n, rows, deep + columns:] = (exact - upper.astype(jnp.float32)).astype(jnp.bfloat16)
        leave(n, slice(deep, deep + 2 * columns))
    for copy in leaving:
        copy.wait()


def project(pattern, counts, exponents, values, matrices, parts, lent):
    kept, terms, owned = pattern.shape
    size = matrices.shape[-1]
    columns = values.shape[1]
    ghosts = parts + 2 * (lent - 1)
    half = jax.ShapeDtypeStruct((terms * columns // 2, ghosts * size + 2 * columns), jnp.bfloat16)
    wide = 8
    return pl.pallas_call(
        functools.partial(project_kernel, parts, lent, owned // 3, wide, terms * columns // parts),
        out_shape=(half, half),
        in_specs=[ANY] * 5,
        out_specs=(ANY, ANY),
        scratch_shapes=[
            pltpu.VMEM((terms * ghosts + 1, columns, size), jnp.float32),
            pltpu.VMEM((owned + 1, size, columns), jnp.bfloat16),
            pltpu.VMEM((owned, columns, size), jnp.bfloat16),
            pltpu.VMEM((2, terms, 4 * size, columns), jnp.bfloat16),
            pltpu.VMEM(matrices.shape, jnp.bfloat16),
            pltpu.VMEM((2,) + half.shape, half.dtype),
            pltpu.VMEM((terms * columns, columns), jnp.float32),
            pltpu.VMEM(values.shape, values.dtype),
            pltpu.VMEM(pattern.shape, jnp.int32),
            pltpu.VMEM(counts.shape, jnp.int32),
            pltpu.VMEM(pattern.shape, jnp.int32),
            pltpu.VMEM(pattern.shape, jnp.int32),
            pltpu.SMEM(pattern.shape, jnp.int32),
            pltpu.SMEM(pattern.shape, jnp.int32),
            pltpu.SMEM(exponents.shape, jnp.int32),
            pltpu.SMEM((owned * terms * kept + 2 * wide,), jnp.int32),
            pltpu.SemaphoreType.DMA((owned // 2,)),
            pltpu.SemaphoreType.DMA((4,)),
            pltpu.SemaphoreType.DMA((2,)),
            pltpu.SemaphoreType.DMA((4,)),
        ],
        compiler_params=pltpu.CompilerParams(vmem_limit_bytes=60 * 2**20),
        cost_estimate=pl.CostEstimate(
            flops=2 * matrices.size * columns, bytes_accessed=2 * matrices.size, transcendentals=0
        ),
        name="project",
    )(pattern, counts, exponents, values, matrices)


def far_kernel(weights, far, out):
    columns = out.shape[1]
    deep = weights.shape[1] - 2 * columns
    total = weights[:, deep:deep + columns].astype(jnp.float32) + weights[:, deep + columns:].astype(jnp.float32)
    out[...] = total + jnp.dot(weights[:, :far.shape[0]], far[...], preferred_element_type=jnp.float32)


def near_kernel(weights, total, far, inner, outer, out):
    start = far.shape[0]
    middle = start + inner.shape[0]
    stop = middle + outer.shape[0]
    near = jnp.dot(weights[:, start:middle], inner[...], preferred_element_type=jnp.float32)
    near += jnp.dot(weights[:, middle:stop], outer[...], preferred_element_type=jnp.float32)
    out[...] = total[...] + near


def half_kernel(weights, far, inner, outer, out):
    far_kernel(weights, far, out)
    near_kernel(weights, out, far, inner, outer, out)


def half_partial(kernel, weights, *blocks):
    rows, columns = weights.shape[0], blocks[-1].shape[1]
    return pl.pallas_call(
        kernel,
        out_shape=jax.ShapeDtypeStruct((rows, columns), jnp.float32),
        in_specs=[VMEM] * (1 + len(blocks)),
        out_specs=VMEM,
        compiler_params=pltpu.CompilerParams(vmem_limit_bytes=4 * 2**20),
        cost_estimate=pl.CostEstimate(
            flops=2 * weights.size * columns, bytes_accessed=2 * weights.size, transcendentals=0
        ),
        name=kernel.__name__,
    )(weights, *blocks)


def on_device(matrices, values, exponents, pattern, block_counts, send_lists, ghost_counts):
    parts = lax.axis_size("dom")
    terms = pattern.shape[0]
    size = matrices.shape[-1]
    lent = send_lists.shape[2]
    row_count, columns = values.shape

    far, inner, outer = pack(jnp.transpose(send_lists, (0, 2, 1)), exponents, values, size)
    mates = [(p, p ^ 1) for p in range(parts)]
    others = [(p, q) for n in range(1, parts - 1, 2) for p, q in ((n, n + 1), (n + 1, n))]
    far = lax.all_to_all(far, "dom", split_axis=0, concat_axis=0, tiled=True)
    outer = lax.ppermute(outer, "dom", others)
    inner = lax.ppermute(inner, "dom", mates)

    send_weights, keep_weights = project(
        jnp.transpose(pattern, (2, 0, 1)), block_counts, exponents, values, matrices, parts, lent
    )
    flat = lambda a: a.reshape(-1, columns)
    far, inner, outer = flat(far), flat(inner), flat(outer)
    send = half_partial(far_kernel, send_weights, far)
    send = half_partial(near_kernel, send_weights, send, far, inner, outer)
    came = lax.ppermute(send, "dom", mates)
    both = came + half_partial(half_kernel, keep_weights, far, inner, outer)
    share = terms * columns // parts
    both = both.astype(jnp.bfloat16).reshape(parts // 2, share, columns)
    groups = [list(range(core, parts, 2)) for core in range(2)]
    pieces = lax.all_to_all(both, "dom", split_axis=0, concat_axis=0, tiled=True, axis_index_groups=groups)
    summed = jnp.sum(pieces.astype(jnp.float32), axis=0)
    return summed * (1.0 / math.sqrt(row_count * parts))


def solution(mesh):
    return jax.shard_map(
        on_device,
        mesh=mesh,
        in_specs=(
            P(None, ("group", "dom"), None, None, None),
            P(("group", "dom"), None),
            P(("group", "dom")),
            P(None, ("group", "dom"), None),
            P(None, ("group", "dom")),
            P(("group", "dom"), None, None),
            P(("group", "dom"), None),
        ),
        out_specs=P(("group", "dom"), None),
        check_vma=False,
    )
```

```python
import functools
import math

import jax
import jax.numpy as jnp
from jax import lax
from jax.experimental import pallas as pl
from jax.experimental.pallas import tpu as pltpu
from jax.sharding import PartitionSpec as P

SMEM = pl.BlockSpec(memory_space=pltpu.SMEM)
VMEM = pl.BlockSpec(memory_space=pltpu.VMEM)
ANY = pl.BlockSpec(memory_space=pl.ANY)


def power_of_two(exponent):
    return (lax.shift_left(jnp.int32(1), exponent + 2).astype(jnp.float32) * 0.25).astype(jnp.bfloat16)


def neighbours(me, parts):
    parity = lax.rem(me, 2)
    return me + 1 - 2 * parity, jnp.clip(me - 1 + 2 * parity, 0, parts - 1)


def pack_kernel(parts, size, lists, exponents, values, far, inner, outer):
    me = lax.axis_index("dom")
    lent = lists.shape[1]
    mate, other = neighbours(me, parts)

    def lend(block, out, n):
        rows = pl.ds(pl.multiple_of(block * size, size), size)
        out[n] = values[rows, :] * power_of_two(exponents[block])

    for p in range(parts):
        lend(lists[0, 0, p], far, p)
    for g in range(1, lent):
        lend(lists[0, g, mate], inner, g - 1)
        lend(lists[0, g, other], outer, g - 1)


def pack(lists, exponents, values, size):
    lent, parts = lists.shape[1:]
    columns = values.shape[1]
    block = lambda n: jax.ShapeDtypeStruct((n, size, columns), values.dtype)
    return pl.pallas_call(
        functools.partial(pack_kernel, parts, size),
        out_shape=(block(parts), block(lent - 1), block(lent - 1)),
        in_specs=[SMEM, SMEM, VMEM],
        out_specs=(VMEM, VMEM, VMEM),
        name="pack",
    )(lists, exponents, values)


def project_kernel(parts, lent, middle, wide, share, pattern_in, counts_in, exponents_in, values_in, matrices, *refs):
    kept, terms, owned = pattern_in.shape
    send_far, send_rest, keep_all = refs[:3]
    (acc, basis, turned, split, held, staged_rest, staged_keep, partial, values, pattern, counts,
     own_table, ghost_table, own_slots, ghost_slots, exponents, listed, came, read, moved, went) = refs[3:]
    me = lax.axis_index("dom")
    size = held.shape[-1]
    columns = values.shape[1]
    mate, _ = neighbours(me, parts)
    ghosts = parts + 2 * (lent - 1)
    trash = terms * ghosts
    steps = owned // 2

    def fetch(step):
        pair = pl.ds(2 * step, 2)
        return pltpu.make_async_copy(matrices.at[:, pair], held.at[:, pair], came.at[step])

    reads = [
        pltpu.make_async_copy(source, target, read.at[n])
        for n, (source, target) in enumerate(
            [(pattern_in, pattern), (counts_in, counts), (exponents_in, exponents), (values_in, values)]
        )
    ]
    for copy in reads:
        copy.start()
    for step in range(2):
        fetch(step).start()

    def clear(n, carry):
        acc[n] = jnp.zeros(acc.shape[1:], acc.dtype)
        return carry

    lax.fori_loop(0, acc.shape[0], clear, 0)
    basis[owned] = jnp.zeros(basis.shape[1:], basis.dtype)
    partial[...] = jnp.zeros(partial.shape, partial.dtype)
    reads[0].wait()
    reads[1].wait()

    slot = pattern[...]
    k, q, b = (lax.broadcasted_iota(jnp.int32, slot.shape, n) for n in range(3))
    present = k < counts[...][None]
    ghost = present & (slot >= owned)
    lender, which = (slot - owned) // lent, (slot - owned) % lent
    further = parts + which - 1 + jnp.where(lender == mate, 0, lent - 1)
    target = q * ghosts + jnp.where(which == 0, lender, further)
    some = jnp.max(ghost.astype(jnp.int32), axis=0, keepdims=True)
    own_table[...] = jnp.where(present & (slot < owned), slot, owned) + jnp.where(k == 0, 256 * some, 0)
    ghost_table[...] = jnp.where(ghost, (1 << 30) + (target << 16) + (b << 8) + (q << 4) + k, 0)
    moves = [
        pltpu.make_async_copy(own_table, own_slots, moved.at[0]),
        pltpu.make_async_copy(ghost_table, ghost_slots, moved.at[1]),
    ]
    for copy in moves:
        copy.start()
    for step in range(2, steps):
        fetch(step).start()
    for copy in moves + reads[2:]:
        copy.wait()

    def prepare(n, found):
        rows = pl.ds(pl.multiple_of(n * size, size), size)
        scaled = values[rows, :] * power_of_two(exponents[n])
        basis[n] = scaled
        turned[n] = scaled.T
        for q in range(terms):
            for k in range(kept):
                word = ghost_slots[k, q, n]
                listed[found] = word
                found += lax.shift_right_logical(word, 30)
        return found

    found = lax.fori_loop(0, owned, prepare, jnp.int32(0))
    for n in range(2 * wide):
        listed[found + n] = trash << 16

    def multiply(step):
        slot = lax.rem(step, 2)
        for sub in range(2):
            b = 2 * step + sub
            for q in range(terms):
                words = [own_slots[k, q, b] for k in range(kept)]
                mixed = lax.shift_right_logical(words[0], 8)
                words[0] = words[0] & 255
                left = jnp.concatenate([held[q, b, k] for k in range(kept)], axis=1)
                table = jnp.concatenate([basis[word] for word in words], axis=0)
                exact = jnp.dot(left, table, preferred_element_type=jnp.float32)
                upper = exact.astype(jnp.bfloat16)
                rest = (exact - upper.astype(jnp.float32)) * mixed.astype(jnp.float32)
                split[slot, q, sub * size:(sub + 1) * size, :] = upper
                split[slot, q, (2 + sub) * size:(3 + sub) * size, :] = rest.astype(jnp.bfloat16)

    def gather(step):
        slot = lax.rem(step, 2)
        left = jnp.concatenate([turned[2 * step], turned[2 * step + 1]] * 2, axis=1)
        for q in range(terms):
            rows = slice(q * columns, (q + 1) * columns)
            partial[rows, :] += jnp.dot(left, split[slot, q], preferred_element_type=jnp.float32)

    def body(step, carry):
        gather(step - 1)
        multiply(step)
        return carry

    def first_body(step, carry):
        fetch(step).wait()
        return body(step, carry)

    fetch(0).wait()
    multiply(jnp.int32(0))
    lax.fori_loop(1, middle, first_body, 0)
    for step in range(middle, steps):
        fetch(step).wait()
    nothing = jnp.zeros((size, size), jnp.bfloat16)

    def take(n):
        word = listed[n]
        field = lambda place, bits: lax.shift_right_logical(word, place) & ((1 << bits) - 1)
        b = field(8, 8)
        return turned[b], held[field(4, 4), b, field(0, 4)], field(16, 14)

    def project_ghosts(n, carry):
        for m in range(wide):
            left_a, block_a, target_a = take(n * 2 * wide + 2 * m)
            left_b, block_b, target_b = take(n * 2 * wide + 2 * m + 1)
            left = jnp.concatenate([left_a, left_b], axis=1)
            right = jnp.concatenate([
                jnp.concatenate([block_a, nothing], axis=1),
                jnp.concatenate([nothing, block_b], axis=1),
            ], axis=0)
            both = jnp.dot(left, right, preferred_element_type=jnp.float32)
            acc[target_a] += both[:, :size]
            acc[target_b] += both[:, size:]
        return carry

    lax.fori_loop(0, lax.div(found + 2 * wide - 1, 2 * wide), project_ghosts, 0)

    parity = lax.rem(me, 2)
    runs = columns // (2 * share)

    def run(m, side):
        return pl.ds(pl.multiple_of((2 * m + side) * share, share), share)

    deep = ghosts * size
    held_slots = send_far.shape[1] // size
    distant = held_slots * size
    leaving = []

    def leave(source, target, lanes):
        leaving.append(pltpu.make_async_copy(source.at[:, lanes], target.at[:, lanes], went.at[len(leaving)]))
        leaving[-1].start()

    def settle(side, first, last, place):
        for q in range(terms):
            for m in range(runs):
                rows = pl.ds((q * runs + m) * share, share)
                for g in range(first, last):
                    lanes = slice((g - first) * size, (g - first + 1) * size)
                    place[rows, lanes] = acc[q * ghosts + g, run(m, side), :].astype(jnp.bfloat16)

    def settle_own(side, start, place):
        for q in range(terms):
            for m in range(runs):
                exact = partial[pl.ds(pl.multiple_of(q * columns + (2 * m + side) * share, share), share), :]
                upper = exact.astype(jnp.bfloat16)
                rows = pl.ds((q * runs + m) * share, share)
                place[rows, start:start + columns] = upper
                place[rows, start + columns:] = (exact - upper.astype(jnp.float32)).astype(jnp.bfloat16)

    settle(parity, 0, ghosts, staged_keep)
    leave(staged_keep, keep_all, slice(0, deep))
    settle(1 - parity, held_slots, ghosts, staged_rest)
    leave(staged_rest, send_rest, slice(0, deep - distant))
    settle(1 - parity, 0, held_slots, send_far)
    lax.fori_loop(middle, steps, body, 0)
    gather(steps - 1)
    settle_own(1 - parity, deep - distant, staged_rest)
    leave(staged_rest, send_rest, slice(deep - distant, deep - distant + 2 * columns))
    settle_own(parity, deep, staged_keep)
    leave(staged_keep, keep_all, slice(deep, deep + 2 * columns))
    for copy in leaving:
        copy.wait()


def project(pattern, counts, exponents, values, matrices, parts, lent):
    kept, terms, owned = pattern.shape
    size = matrices.shape[-1]
    columns = values.shape[1]
    ghosts = parts + 2 * (lent - 1)
    half = lambda lanes: jax.ShapeDtypeStruct((terms * columns // 2, lanes), jnp.bfloat16)
    held_slots = parts * 6 // 16
    far = half(held_slots * size)
    rest = half((ghosts - held_slots) * size + 2 * columns)
    keep = half(ghosts * size + 2 * columns)
    wide = 8
    rooms = [
        ((terms * ghosts + 1, columns, size), jnp.float32),
        ((owned + 1, size, columns), jnp.bfloat16),
        ((owned, columns, size), jnp.bfloat16),
        ((2, terms, 4 * size, columns), jnp.bfloat16),
        (matrices.shape, jnp.bfloat16),
        (rest.shape, rest.dtype),
        (keep.shape, keep.dtype),
        ((terms * columns, columns), jnp.float32),
        (values.shape, values.dtype),
    ]
    needed = sum(math.prod(shape) * jnp.dtype(dtype).itemsize for shape, dtype in rooms)
    grant = max(52 * 2**20, needed + 4 * 2**20)
    return pl.pallas_call(
        functools.partial(project_kernel, parts, lent, owned // 3, wide, terms * columns // parts),
        out_shape=(far, rest, keep),
        in_specs=[ANY] * 5,
        out_specs=(VMEM, ANY, ANY),
        scratch_shapes=[pltpu.VMEM(*room) for room in rooms] + [
            pltpu.VMEM(pattern.shape, jnp.int32),
            pltpu.VMEM(counts.shape, jnp.int32),
            pltpu.VMEM(pattern.shape, jnp.int32),
            pltpu.VMEM(pattern.shape, jnp.int32),
            pltpu.SMEM(pattern.shape, jnp.int32),
            pltpu.SMEM(pattern.shape, jnp.int32),
            pltpu.SMEM(exponents.shape, jnp.int32),
            pltpu.SMEM((owned * terms * kept + 2 * wide,), jnp.int32),
            pltpu.SemaphoreType.DMA((owned // 2,)),
            pltpu.SemaphoreType.DMA((4,)),
            pltpu.SemaphoreType.DMA((2,)),
            pltpu.SemaphoreType.DMA((4,)),
        ],
        compiler_params=pltpu.CompilerParams(vmem_limit_bytes=grant),
        cost_estimate=pl.CostEstimate(
            flops=2 * matrices.size * columns, bytes_accessed=2 * matrices.size, transcendentals=0
        ),
        name="project",
    )(pattern, counts, exponents, values, matrices)


def whole(ref):
    columns = ref.shape[1] // 2
    return ref[:, :columns].astype(jnp.float32) + ref[:, columns:].astype(jnp.float32)


def far_kernel(weights, far, out):
    out[...] = jnp.dot(weights[...], far[:weights.shape[1], :], preferred_element_type=jnp.float32)


def near_kernel(done, total, weights, far, inner, outer, out):
    result = total[...] + whole(weights.at[:, weights.shape[1] - 2 * out.shape[1]:])
    start = 0
    for block in (far.at[done:, :], inner, outer):
        stop = start + block.shape[0]
        result += jnp.dot(weights[:, start:stop], block[...], preferred_element_type=jnp.float32)
        start = stop
    out[...] = result


def half_kernel(weights, far, inner, outer, out):
    total = whole(weights.at[:, weights.shape[1] - 2 * out.shape[1]:])
    start = 0
    for block in (far, inner, outer):
        stop = start + block.shape[0]
        total += jnp.dot(weights[:, start:stop], block[...], preferred_element_type=jnp.float32)
        start = stop
    out[...] = total


def half_partial(name, kernel, *arrays):
    rows, columns = arrays[0].shape[0], arrays[-1].shape[1]
    return pl.pallas_call(
        kernel,
        out_shape=jax.ShapeDtypeStruct((rows, columns), jnp.float32),
        in_specs=[VMEM] * len(arrays),
        out_specs=VMEM,
        compiler_params=pltpu.CompilerParams(vmem_limit_bytes=4 * 2**20),
        cost_estimate=pl.CostEstimate(
            flops=2 * rows * columns * 4096, bytes_accessed=sum(a.size * 2 for a in arrays), transcendentals=0
        ),
        name=name,
    )(*arrays)


def on_device(matrices, values, exponents, pattern, block_counts, send_lists, ghost_counts):
    parts = lax.axis_size("dom")
    terms = pattern.shape[0]
    size = matrices.shape[-1]
    lent = send_lists.shape[2]
    row_count, columns = values.shape

    far, inner, outer = pack(jnp.transpose(send_lists, (0, 2, 1)), exponents, values, size)
    mates = [(p, p ^ 1) for p in range(parts)]
    others = [(p, q) for n in range(1, parts - 1, 2) for p, q in ((n, n + 1), (n + 1, n))]
    far = lax.all_to_all(far, "dom", split_axis=0, concat_axis=0, tiled=True)
    outer = lax.ppermute(outer, "dom", others)
    inner = lax.ppermute(inner, "dom", mates)

    far_weights, rest_weights, weights = project(
        jnp.transpose(pattern, (2, 0, 1)), block_counts, exponents, values, matrices, parts, lent
    )
    flat = lambda a: a.reshape(-1, columns)
    far, inner, outer = flat(far), flat(inner), flat(outer)
    send = half_partial("far", far_kernel, far_weights, far)
    send = half_partial(
        "near", functools.partial(near_kernel, far_weights.shape[1]), send, rest_weights, far, inner, outer
    )
    came = lax.ppermute(send, "dom", mates)
    both = came + half_partial("half", half_kernel, weights, far, inner, outer)
    share = terms * columns // parts
    both = both.astype(jnp.bfloat16).reshape(parts // 2, share, columns)
    groups = [list(range(core, parts, 2)) for core in range(2)]
    pieces = lax.all_to_all(both, "dom", split_axis=0, concat_axis=0, tiled=True, axis_index_groups=groups)
    summed = jnp.sum(pieces.astype(jnp.float32), axis=0)
    return summed * (1.0 / math.sqrt(row_count * parts))


def solution(mesh):
    return jax.shard_map(
        on_device,
        mesh=mesh,
        in_specs=(
            P(None, ("group", "dom"), None, None, None),
            P(("group", "dom"), None),
            P(("group", "dom")),
            P(None, ("group", "dom"), None),
            P(None, ("group", "dom")),
            P(("group", "dom"), None, None),
            P(("group", "dom"), None),
        ),
        out_specs=P(("group", "dom"), None),
        check_vma=False,
    )
```

```python
import functools
import math

import jax
import jax.numpy as jnp
from jax import lax
from jax.experimental import pallas as pl
from jax.experimental.pallas import tpu as pltpu
from jax.sharding import PartitionSpec as P

SMEM = pl.BlockSpec(memory_space=pltpu.SMEM)
VMEM = pl.BlockSpec(memory_space=pltpu.VMEM)
ANY = pl.BlockSpec(memory_space=pl.ANY)


def power_of_two(exponent):
    return (lax.shift_left(jnp.int32(1), exponent + 2).astype(jnp.float32) * 0.25).astype(jnp.bfloat16)


def neighbours(me, parts):
    parity = lax.rem(me, 2)
    return me + 1 - 2 * parity, jnp.clip(me - 1 + 2 * parity, 0, parts - 1)


def pack_kernel(parts, size, lists, exponents, values, far, inner, outer):
    me = lax.axis_index("dom")
    lent = lists.shape[1]
    mate, other = neighbours(me, parts)

    def lend(block, out, n):
        rows = pl.ds(pl.multiple_of(block * size, size), size)
        out[n] = values[rows, :] * power_of_two(exponents[block])

    for p in range(parts):
        lend(lists[0, 0, p], far, p)
    for g in range(1, lent):
        lend(lists[0, g, mate], inner, g - 1)
        lend(lists[0, g, other], outer, g - 1)


def pack(lists, exponents, values, size):
    lent, parts = lists.shape[1:]
    columns = values.shape[1]
    block = lambda n: jax.ShapeDtypeStruct((n, size, columns), values.dtype)
    return pl.pallas_call(
        functools.partial(pack_kernel, parts, size),
        out_shape=(block(parts), block(lent - 1), block(lent - 1)),
        in_specs=[SMEM, SMEM, VMEM],
        out_specs=(VMEM, VMEM, VMEM),
        name="pack",
    )(lists, exponents, values)


def project_kernel(parts, lent, middle, wide, share, pattern_in, counts_in, exponents_in, values_in, matrices, *refs):
    kept, terms, owned = pattern_in.shape
    send_far, send_rest, keep_all = refs[:3]
    (acc, basis, turned, split, held, staged_rest, staged_keep, partial, values, pattern, counts,
     own_table, ghost_table, own_slots, ghost_slots, exponents, listed, came, read, moved, went) = refs[3:]
    me = lax.axis_index("dom")
    size = held.shape[-1]
    columns = values.shape[1]
    mate, _ = neighbours(me, parts)
    ghosts = parts + 2 * (lent - 1)
    trash = terms * ghosts
    steps = owned // 2

    def fetch(step):
        pair = pl.ds(2 * step, 2)
        return pltpu.make_async_copy(matrices.at[:, pair], held.at[:, pair], came.at[step])

    reads = [
        pltpu.make_async_copy(source, target, read.at[n])
        for n, (source, target) in enumerate(
            [(pattern_in, pattern), (counts_in, counts), (exponents_in, exponents), (values_in, values)]
        )
    ]
    for copy in reads:
        copy.start()
    for step in range(2):
        fetch(step).start()

    def clear(n, carry):
        acc[n] = jnp.zeros(acc.shape[1:], acc.dtype)
        return carry

    lax.fori_loop(0, acc.shape[0], clear, 0)
    basis[owned] = jnp.zeros(basis.shape[1:], basis.dtype)
    partial[...] = jnp.zeros(partial.shape, partial.dtype)
    reads[0].wait()
    reads[1].wait()

    slot = pattern[...]
    k, q, b = (lax.broadcasted_iota(jnp.int32, slot.shape, n) for n in range(3))
    present = k < counts[...][None]
    ghost = present & (slot >= owned)
    lender, which = (slot - owned) // lent, (slot - owned) % lent
    further = parts + which - 1 + jnp.where(lender == mate, 0, lent - 1)
    target = q * ghosts + jnp.where(which == 0, lender, further)
    some = jnp.max(ghost.astype(jnp.int32), axis=0, keepdims=True)
    own_table[...] = jnp.where(present & (slot < owned), slot, owned) + jnp.where(k == 0, 256 * some, 0)
    ghost_table[...] = jnp.where(ghost, (1 << 30) + (target << 16) + (b << 8) + (q << 4) + k, 0)
    moves = [
        pltpu.make_async_copy(own_table, own_slots, moved.at[0]),
        pltpu.make_async_copy(ghost_table, ghost_slots, moved.at[1]),
    ]
    for copy in moves:
        copy.start()
    for step in range(2, steps):
        fetch(step).start()
    for copy in moves + reads[2:]:
        copy.wait()

    def prepare(n, found):
        rows = pl.ds(pl.multiple_of(n * size, size), size)
        scaled = values[rows, :] * power_of_two(exponents[n])
        basis[n] = scaled
        turned[n] = scaled.T
        for q in range(terms):
            for k in range(kept):
                word = ghost_slots[k, q, n]
                listed[found] = word
                found += lax.shift_right_logical(word, 30)
        return found

    found = lax.fori_loop(0, owned, prepare, jnp.int32(0))
    for n in range(2 * wide):
        listed[found + n] = trash << 16

    def multiply(step):
        slot = lax.rem(step, 2)
        for sub in range(2):
            b = 2 * step + sub
            for q in range(terms):
                words = [own_slots[k, q, b] for k in range(kept)]
                mixed = lax.shift_right_logical(words[0], 8)
                words[0] = words[0] & 255
                left = jnp.concatenate([held[q, b, k] for k in range(kept)], axis=1)
                table = jnp.concatenate([basis[word] for word in words], axis=0)
                exact = jnp.dot(left, table, preferred_element_type=jnp.float32)
                upper = exact.astype(jnp.bfloat16)
                rest = (exact - upper.astype(jnp.float32)) * mixed.astype(jnp.float32)
                split[slot, q, sub * size:(sub + 1) * size, :] = upper
                split[slot, q, (2 + sub) * size:(3 + sub) * size, :] = rest.astype(jnp.bfloat16)

    def gather(step):
        slot = lax.rem(step, 2)
        left = jnp.concatenate([turned[2 * step], turned[2 * step + 1]] * 2, axis=1)
        for q in range(terms):
            rows = slice(q * columns, (q + 1) * columns)
            partial[rows, :] += jnp.dot(left, split[slot, q], preferred_element_type=jnp.float32)

    def body(step, carry):
        gather(step - 1)
        multiply(step)
        return carry

    def first_body(step, carry):
        fetch(step).wait()
        return body(step, carry)

    fetch(0).wait()
    multiply(jnp.int32(0))
    lax.fori_loop(1, middle, first_body, 0)
    for step in range(middle, steps):
        fetch(step).wait()
    nothing = jnp.zeros((size, size), jnp.bfloat16)

    def take(n):
        word = listed[n]
        field = lambda place, bits: lax.shift_right_logical(word, place) & ((1 << bits) - 1)
        b = field(8, 8)
        return turned[b], held[field(4, 4), b, field(0, 4)], field(16, 14)

    def project_ghosts(n, carry):
        for m in range(wide):
            left_a, block_a, target_a = take(n * 2 * wide + 2 * m)
            left_b, block_b, target_b = take(n * 2 * wide + 2 * m + 1)
            left = jnp.concatenate([left_a, left_b], axis=1)
            right = jnp.concatenate([
                jnp.concatenate([block_a, nothing], axis=1),
                jnp.concatenate([nothing, block_b], axis=1),
            ], axis=0)
            both = jnp.dot(left, right, preferred_element_type=jnp.float32)
            acc[target_a] += both[:, :size]
            acc[target_b] += both[:, size:]
        return carry

    lax.fori_loop(0, lax.div(found + 2 * wide - 1, 2 * wide), project_ghosts, 0)

    parity = lax.rem(me, 2)
    runs = columns // (2 * share)

    def run(m, side):
        return pl.ds(pl.multiple_of((2 * m + side) * share, share), share)

    deep = ghosts * size
    held_slots = send_far.shape[1] // size
    distant = held_slots * size
    leaving = []

    def leave(source, target, lanes):
        leaving.append(pltpu.make_async_copy(source.at[:, lanes], target.at[:, lanes], went.at[len(leaving)]))
        leaving[-1].start()

    def settle(side, first, last, place):
        for q in range(terms):
            for m in range(runs):
                rows = pl.ds((q * runs + m) * share, share)
                for g in range(first, last):
                    lanes = slice((g - first) * size, (g - first + 1) * size)
                    place[rows, lanes] = acc[q * ghosts + g, run(m, side), :].astype(jnp.bfloat16)

    def settle_own(side, start, place):
        for q in range(terms):
            for m in range(runs):
                exact = partial[pl.ds(pl.multiple_of(q * columns + (2 * m + side) * share, share), share), :]
                upper = exact.astype(jnp.bfloat16)
                rows = pl.ds((q * runs + m) * share, share)
                place[rows, start:start + columns] = upper
                place[rows, start + columns:] = (exact - upper.astype(jnp.float32)).astype(jnp.bfloat16)

    settle(parity, 0, ghosts, staged_keep)
    leave(staged_keep, keep_all, slice(0, deep))
    settle(1 - parity, held_slots, ghosts, staged_rest)
    leave(staged_rest, send_rest, slice(0, deep - distant))
    settle(1 - parity, 0, held_slots, send_far)
    lax.fori_loop(middle, steps, body, 0)
    gather(steps - 1)
    settle_own(1 - parity, deep - distant, staged_rest)
    leave(staged_rest, send_rest, slice(deep - distant, deep - distant + 2 * columns))
    settle_own(parity, deep, staged_keep)
    leave(staged_keep, keep_all, slice(deep, deep + 2 * columns))
    for copy in leaving:
        copy.wait()


def project(pattern, counts, exponents, values, matrices, parts, lent):
    kept, terms, owned = pattern.shape
    size = matrices.shape[-1]
    columns = values.shape[1]
    ghosts = parts + 2 * (lent - 1)
    half = lambda lanes: jax.ShapeDtypeStruct((terms * columns // 2, lanes), jnp.bfloat16)
    held_slots = parts * 6 // 16
    far = half(held_slots * size)
    rest = half((ghosts - held_slots) * size + 2 * columns)
    keep = half(ghosts * size + 2 * columns)
    wide = 8
    rooms = [
        ((terms * ghosts + 1, columns, size), jnp.float32),
        ((owned + 1, size, columns), jnp.bfloat16),
        ((owned, columns, size), jnp.bfloat16),
        ((2, terms, 4 * size, columns), jnp.bfloat16),
        (matrices.shape, jnp.bfloat16),
        (rest.shape, rest.dtype),
        (keep.shape, keep.dtype),
        ((terms * columns, columns), jnp.float32),
        (values.shape, values.dtype),
    ]
    needed = sum(math.prod(shape) * jnp.dtype(dtype).itemsize for shape, dtype in rooms)
    grant = max(52 * 2**20, needed + 4 * 2**20)
    return pl.pallas_call(
        functools.partial(project_kernel, parts, lent, owned // 3, wide, terms * columns // parts),
        out_shape=(far, rest, keep),
        in_specs=[ANY] * 5,
        out_specs=(VMEM, ANY, ANY),
        scratch_shapes=[pltpu.VMEM(*room) for room in rooms] + [
            pltpu.VMEM(pattern.shape, jnp.int32),
            pltpu.VMEM(counts.shape, jnp.int32),
            pltpu.VMEM(pattern.shape, jnp.int32),
            pltpu.VMEM(pattern.shape, jnp.int32),
            pltpu.SMEM(pattern.shape, jnp.int32),
            pltpu.SMEM(pattern.shape, jnp.int32),
            pltpu.SMEM(exponents.shape, jnp.int32),
            pltpu.SMEM((owned * terms * kept + 2 * wide,), jnp.int32),
            pltpu.SemaphoreType.DMA((owned // 2,)),
            pltpu.SemaphoreType.DMA((4,)),
            pltpu.SemaphoreType.DMA((2,)),
            pltpu.SemaphoreType.DMA((4,)),
        ],
        compiler_params=pltpu.CompilerParams(vmem_limit_bytes=grant),
        cost_estimate=pl.CostEstimate(
            flops=2 * matrices.size * columns, bytes_accessed=2 * matrices.size, transcendentals=0
        ),
        name="project",
    )(pattern, counts, exponents, values, matrices)


def whole(ref):
    columns = ref.shape[1] // 2
    return ref[:, :columns].astype(jnp.float32) + ref[:, columns:].astype(jnp.float32)


def far_kernel(weights, far, out):
    out[...] = jnp.dot(weights[...], far[:weights.shape[1], :], preferred_element_type=jnp.float32)


def near_kernel(done, total, weights, far, inner, outer, out):
    result = total[...] + whole(weights.at[:, weights.shape[1] - 2 * out.shape[1]:])
    start = 0
    for block in (far.at[done:, :], inner, outer):
        stop = start + block.shape[0]
        result += jnp.dot(weights[:, start:stop], block[...], preferred_element_type=jnp.float32)
        start = stop
    out[...] = result


def half_kernel(weights, far, inner, outer, out):
    total = whole(weights.at[:, weights.shape[1] - 2 * out.shape[1]:])
    start = 0
    for block in (far, inner, outer):
        stop = start + block.shape[0]
        total += jnp.dot(weights[:, start:stop], block[...], preferred_element_type=jnp.float32)
        start = stop
    out[...] = total


def half_partial(name, kernel, *arrays):
    rows, columns = arrays[0].shape[0], arrays[-1].shape[1]
    return pl.pallas_call(
        kernel,
        out_shape=jax.ShapeDtypeStruct((rows, columns), jnp.float32),
        in_specs=[VMEM] * len(arrays),
        out_specs=VMEM,
        compiler_params=pltpu.CompilerParams(vmem_limit_bytes=4 * 2**20),
        cost_estimate=pl.CostEstimate(
            flops=2 * rows * columns * 4096, bytes_accessed=sum(a.size * 2 for a in arrays), transcendentals=0
        ),
        name=name,
    )(*arrays)


def on_device(matrices, values, exponents, pattern, block_counts, send_lists, ghost_counts):
    parts = lax.axis_size("dom")
    terms = pattern.shape[0]
    size = matrices.shape[-1]
    lent = send_lists.shape[2]
    row_count, columns = values.shape

    far, inner, outer = pack(jnp.transpose(send_lists, (0, 2, 1)), exponents, values, size)
    mates = [(p, p ^ 1) for p in range(parts)]
    others = [(p, q) for n in range(1, parts - 1, 2) for p, q in ((n, n + 1), (n + 1, n))]
    far = lax.all_to_all(far, "dom", split_axis=0, concat_axis=0, tiled=True)
    outer = lax.ppermute(outer, "dom", others)

    far_weights, rest_weights, weights = project(
        jnp.transpose(pattern, (2, 0, 1)), block_counts, exponents, values, matrices, parts, lent
    )
    inner, far_weights, rest_weights, weights = lax.optimization_barrier((inner, far_weights, rest_weights, weights))
    inner = lax.ppermute(inner, "dom", mates)
    flat = lambda a: a.reshape(-1, columns)
    far, inner, outer = flat(far), flat(inner), flat(outer)
    send = half_partial("far", far_kernel, far_weights, far)
    send = half_partial(
        "near", functools.partial(near_kernel, far_weights.shape[1]), send, rest_weights, far, inner, outer
    )
    came = lax.ppermute(send, "dom", mates)
    both = came + half_partial("half", half_kernel, weights, far, inner, outer)
    share = terms * columns // parts
    both = both.astype(jnp.bfloat16).reshape(parts // 2, share, columns)
    groups = [list(range(core, parts, 2)) for core in range(2)]
    pieces = lax.all_to_all(both, "dom", split_axis=0, concat_axis=0, tiled=True, axis_index_groups=groups)
    summed = jnp.sum(pieces.astype(jnp.float32), axis=0)
    return summed * (1.0 / math.sqrt(row_count * parts))


def solution(mesh):
    return jax.shard_map(
        on_device,
        mesh=mesh,
        in_specs=(
            P(None, ("group", "dom"), None, None, None),
            P(("group", "dom"), None),
            P(("group", "dom")),
            P(None, ("group", "dom"), None),
            P(None, ("group", "dom")),
            P(("group", "dom"), None, None),
            P(("group", "dom"), None),
        ),
        out_specs=P(("group", "dom"), None),
        check_vma=False,
    )
```

```python
import functools
import math

import jax
import jax.numpy as jnp
from jax import lax
from jax.experimental import pallas as pl
from jax.experimental.pallas import tpu as pltpu
from jax.sharding import PartitionSpec as P

SMEM = pl.BlockSpec(memory_space=pltpu.SMEM)
VMEM = pl.BlockSpec(memory_space=pltpu.VMEM)
ANY = pl.BlockSpec(memory_space=pl.ANY)


def power_of_two(exponent):
    return (lax.shift_left(jnp.int32(1), exponent + 2).astype(jnp.float32) * 0.25).astype(jnp.bfloat16)


def neighbours(me, parts):
    parity = lax.rem(me, 2)
    return me + 1 - 2 * parity, jnp.clip(me - 1 + 2 * parity, 0, parts - 1)


def pack_kernel(parts, size, lists, exponents, values, far, inner, outer):
    me = lax.axis_index("dom")
    lent = lists.shape[1]
    mate, other = neighbours(me, parts)

    def lend(block, out, n):
        rows = pl.ds(pl.multiple_of(block * size, size), size)
        out[n] = values[rows, :] * power_of_two(exponents[block])

    for p in range(parts):
        lend(lists[0, 0, p], far, p)
    for g in range(1, lent):
        lend(lists[0, g, mate], inner, g - 1)
        lend(lists[0, g, other], outer, g - 1)


def pack(lists, exponents, values, size):
    lent, parts = lists.shape[1:]
    columns = values.shape[1]
    block = lambda n: jax.ShapeDtypeStruct((n, size, columns), values.dtype)
    return pl.pallas_call(
        functools.partial(pack_kernel, parts, size),
        out_shape=(block(parts), block(lent - 1), block(lent - 1)),
        in_specs=[SMEM, SMEM, VMEM],
        out_specs=(VMEM, VMEM, VMEM),
        name="pack",
    )(lists, exponents, values)


def project_kernel(parts, lent, middle, wide, share, pattern_in, counts_in, exponents_in, values_in, matrices, *refs):
    kept, terms, owned = pattern_in.shape
    send_far, send_rest, keep_all = refs[:3]
    (acc, basis, turned, split, held, staged_rest, staged_keep, partial, values, pattern, counts,
     own_table, ghost_table, own_slots, ghost_slots, exponents, listed, came, read, moved, went) = refs[3:]
    me = lax.axis_index("dom")
    size = held.shape[-1]
    columns = values.shape[1]
    mate, _ = neighbours(me, parts)
    ghosts = parts + 2 * (lent - 1)
    trash = terms * ghosts
    steps = owned // 2

    def fetch(step):
        pair = pl.ds(2 * step, 2)
        return pltpu.make_async_copy(matrices.at[:, pair], held.at[:, pair], came.at[step])

    reads = [
        pltpu.make_async_copy(source, target, read.at[n])
        for n, (source, target) in enumerate(
            [(pattern_in, pattern), (counts_in, counts), (exponents_in, exponents), (values_in, values)]
        )
    ]
    for copy in reads:
        copy.start()
    for step in range(2):
        fetch(step).start()

    def clear(n, carry):
        acc[n] = jnp.zeros(acc.shape[1:], acc.dtype)
        return carry

    lax.fori_loop(0, acc.shape[0], clear, 0)
    basis[owned] = jnp.zeros(basis.shape[1:], basis.dtype)
    partial[...] = jnp.zeros(partial.shape, partial.dtype)
    reads[0].wait()
    reads[1].wait()

    slot = pattern[...]
    k, q, b = (lax.broadcasted_iota(jnp.int32, slot.shape, n) for n in range(3))
    present = k < counts[...][None]
    ghost = present & (slot >= owned)
    lender, which = (slot - owned) // lent, (slot - owned) % lent
    further = parts + which - 1 + jnp.where(lender == mate, 0, lent - 1)
    target = q * ghosts + jnp.where(which == 0, lender, further)
    some = jnp.max(ghost.astype(jnp.int32), axis=0, keepdims=True)
    own_table[...] = jnp.where(present & (slot < owned), slot, owned) + jnp.where(k == 0, 256 * some, 0)
    ghost_table[...] = jnp.where(ghost, (1 << 30) + (target << 16) + (b << 8) + (q << 4) + k, 0)
    moves = [
        pltpu.make_async_copy(own_table, own_slots, moved.at[0]),
        pltpu.make_async_copy(ghost_table, ghost_slots, moved.at[1]),
    ]
    for copy in moves:
        copy.start()
    for step in range(2, steps):
        fetch(step).start()
    for copy in moves + reads[2:]:
        copy.wait()

    def prepare(n, found):
        rows = pl.ds(pl.multiple_of(n * size, size), size)
        scaled = values[rows, :] * power_of_two(exponents[n])
        basis[n] = scaled
        turned[n] = scaled.T
        for q in range(terms):
            for k in range(kept):
                word = ghost_slots[k, q, n]
                listed[found] = word
                found += lax.shift_right_logical(word, 30)
        return found

    found = lax.fori_loop(0, owned, prepare, jnp.int32(0))
    for n in range(2 * wide):
        listed[found + n] = trash << 16

    def multiply(step):
        slot = lax.rem(step, 2)
        for sub in range(2):
            b = 2 * step + sub
            for q in range(terms):
                words = [own_slots[k, q, b] for k in range(kept)]
                mixed = lax.shift_right_logical(words[0], 8)
                words[0] = words[0] & 255
                left = jnp.concatenate([held[q, b, k] for k in range(kept)], axis=1)
                table = jnp.concatenate([basis[word] for word in words], axis=0)
                exact = jnp.dot(left, table, preferred_element_type=jnp.float32)
                upper = exact.astype(jnp.bfloat16)
                rest = (exact - upper.astype(jnp.float32)) * mixed.astype(jnp.float32)
                split[slot, q, sub * size:(sub + 1) * size, :] = upper
                split[slot, q, (2 + sub) * size:(3 + sub) * size, :] = rest.astype(jnp.bfloat16)

    def gather(step):
        slot = lax.rem(step, 2)
        left = jnp.concatenate([turned[2 * step], turned[2 * step + 1]] * 2, axis=1)
        for q in range(terms):
            rows = slice(q * columns, (q + 1) * columns)
            partial[rows, :] += jnp.dot(left, split[slot, q], preferred_element_type=jnp.float32)

    def body(step, carry):
        gather(step - 1)
        multiply(step)
        return carry

    def first_body(step, carry):
        fetch(step).wait()
        return body(step, carry)

    fetch(0).wait()
    multiply(jnp.int32(0))
    lax.fori_loop(1, middle, first_body, 0)
    for step in range(middle, steps):
        fetch(step).wait()
    nothing = jnp.zeros((size, size), jnp.bfloat16)

    def take(n):
        word = listed[n]
        field = lambda place, bits: lax.shift_right_logical(word, place) & ((1 << bits) - 1)
        b = field(8, 8)
        return turned[b], held[field(4, 4), b, field(0, 4)], field(16, 14)

    def project_ghosts(n, carry):
        for m in range(wide):
            left_a, block_a, target_a = take(n * 2 * wide + 2 * m)
            left_b, block_b, target_b = take(n * 2 * wide + 2 * m + 1)
            left = jnp.concatenate([left_a, left_b], axis=1)
            right = jnp.concatenate([
                jnp.concatenate([block_a, nothing], axis=1),
                jnp.concatenate([nothing, block_b], axis=1),
            ], axis=0)
            both = jnp.dot(left, right, preferred_element_type=jnp.float32)
            acc[target_a] += both[:, :size]
            acc[target_b] += both[:, size:]
        return carry

    lax.fori_loop(0, lax.div(found + 2 * wide - 1, 2 * wide), project_ghosts, 0)

    parity = lax.rem(me, 2)
    runs = columns // (2 * share)

    def run(m, side):
        return pl.ds(pl.multiple_of((2 * m + side) * share, share), share)

    deep = ghosts * size
    held_slots = send_far.shape[1] // size
    distant = held_slots * size
    leaving = []

    def leave(source, target, lanes):
        leaving.append(pltpu.make_async_copy(source.at[:, lanes], target.at[:, lanes], went.at[len(leaving)]))
        leaving[-1].start()

    def settle(side, first, last, place):
        for q in range(terms):
            for m in range(runs):
                rows = pl.ds((q * runs + m) * share, share)
                for g in range(first, last):
                    lanes = slice((g - first) * size, (g - first + 1) * size)
                    place[rows, lanes] = acc[q * ghosts + g, run(m, side), :].astype(jnp.bfloat16)

    def settle_own(side, start, place):
        for q in range(terms):
            for m in range(runs):
                exact = partial[pl.ds(pl.multiple_of(q * columns + (2 * m + side) * share, share), share), :]
                upper = exact.astype(jnp.bfloat16)
                rows = pl.ds((q * runs + m) * share, share)
                place[rows, start:start + columns] = upper
                place[rows, start + columns:] = (exact - upper.astype(jnp.float32)).astype(jnp.bfloat16)

    settle(parity, 0, ghosts, staged_keep)
    leave(staged_keep, keep_all, slice(0, deep))
    settle(1 - parity, held_slots, ghosts, staged_rest)
    leave(staged_rest, send_rest, slice(0, deep - distant))
    settle(1 - parity, 0, held_slots, send_far)
    lax.fori_loop(middle, steps, body, 0)
    gather(steps - 1)
    settle_own(1 - parity, deep - distant, staged_rest)
    leave(staged_rest, send_rest, slice(deep - distant, deep - distant + 2 * columns))
    settle_own(parity, deep, staged_keep)
    leave(staged_keep, keep_all, slice(deep, deep + 2 * columns))
    for copy in leaving:
        copy.wait()


def project(pattern, counts, exponents, values, matrices, parts, lent):
    kept, terms, owned = pattern.shape
    size = matrices.shape[-1]
    columns = values.shape[1]
    ghosts = parts + 2 * (lent - 1)
    half = lambda lanes: jax.ShapeDtypeStruct((terms * columns // 2, lanes), jnp.bfloat16)
    held_slots = parts * 6 // 16
    far = half(held_slots * size)
    rest = half((ghosts - held_slots) * size + 2 * columns)
    keep = half(ghosts * size + 2 * columns)
    wide = 8
    rooms = [
        ((terms * ghosts + 1, columns, size), jnp.float32),
        ((owned + 1, size, columns), jnp.bfloat16),
        ((owned, columns, size), jnp.bfloat16),
        ((2, terms, 4 * size, columns), jnp.bfloat16),
        (matrices.shape, jnp.bfloat16),
        (rest.shape, rest.dtype),
        (keep.shape, keep.dtype),
        ((terms * columns, columns), jnp.float32),
        (values.shape, values.dtype),
    ]
    needed = sum(math.prod(shape) * jnp.dtype(dtype).itemsize for shape, dtype in rooms)
    grant = max(52 * 2**20, needed + 4 * 2**20)
    return pl.pallas_call(
        functools.partial(project_kernel, parts, lent, owned // 3, wide, terms * columns // parts),
        out_shape=(far, rest, keep),
        in_specs=[ANY] * 5,
        out_specs=(VMEM, ANY, ANY),
        scratch_shapes=[pltpu.VMEM(*room) for room in rooms] + [
            pltpu.VMEM(pattern.shape, jnp.int32),
            pltpu.VMEM(counts.shape, jnp.int32),
            pltpu.VMEM(pattern.shape, jnp.int32),
            pltpu.VMEM(pattern.shape, jnp.int32),
            pltpu.SMEM(pattern.shape, jnp.int32),
            pltpu.SMEM(pattern.shape, jnp.int32),
            pltpu.SMEM(exponents.shape, jnp.int32),
            pltpu.SMEM((owned * terms * kept + 2 * wide,), jnp.int32),
            pltpu.SemaphoreType.DMA((owned // 2,)),
            pltpu.SemaphoreType.DMA((4,)),
            pltpu.SemaphoreType.DMA((2,)),
            pltpu.SemaphoreType.DMA((4,)),
        ],
        compiler_params=pltpu.CompilerParams(vmem_limit_bytes=grant),
        cost_estimate=pl.CostEstimate(
            flops=2 * matrices.size * columns, bytes_accessed=2 * matrices.size, transcendentals=0
        ),
        name="project",
    )(pattern, counts, exponents, values, matrices)


def whole(ref):
    columns = ref.shape[1] // 2
    return ref[:, :columns].astype(jnp.float32) + ref[:, columns:].astype(jnp.float32)


def far_kernel(weights, far, out):
    out[...] = jnp.dot(weights[...], far[:weights.shape[1], :], preferred_element_type=jnp.float32)


def near_kernel(done, total, weights, far, inner, outer, out):
    result = total[...] + whole(weights.at[:, weights.shape[1] - 2 * out.shape[1]:])
    start = 0
    for block in (far.at[done:, :], inner, outer):
        stop = start + block.shape[0]
        result += jnp.dot(weights[:, start:stop], block[...], preferred_element_type=jnp.float32)
        start = stop
    out[...] = result


def half_kernel(weights, far, inner, outer, out):
    total = whole(weights.at[:, weights.shape[1] - 2 * out.shape[1]:])
    start = 0
    for block in (far, inner, outer):
        stop = start + block.shape[0]
        total += jnp.dot(weights[:, start:stop], block[...], preferred_element_type=jnp.float32)
        start = stop
    out[...] = total


def half_partial(name, kernel, *arrays):
    rows, columns = arrays[0].shape[0], arrays[-1].shape[1]
    return pl.pallas_call(
        kernel,
        out_shape=jax.ShapeDtypeStruct((rows, columns), jnp.float32),
        in_specs=[VMEM] * len(arrays),
        out_specs=VMEM,
        compiler_params=pltpu.CompilerParams(vmem_limit_bytes=4 * 2**20),
        cost_estimate=pl.CostEstimate(
            flops=2 * rows * columns * 4096, bytes_accessed=sum(a.size * 2 for a in arrays), transcendentals=0
        ),
        name=name,
    )(*arrays)


def on_device(matrices, values, exponents, pattern, block_counts, send_lists, ghost_counts):
    parts = lax.axis_size("dom")
    terms = pattern.shape[0]
    size = matrices.shape[-1]
    lent = send_lists.shape[2]
    row_count, columns = values.shape

    far, inner, outer = pack(jnp.transpose(send_lists, (0, 2, 1)), exponents, values, size)
    mates = [(p, p ^ 1) for p in range(parts)]
    others = [(p, q) for n in range(1, parts - 1, 2) for p, q in ((n, n + 1), (n + 1, n))]
    far = lax.all_to_all(far, "dom", split_axis=0, concat_axis=0, tiled=True)
    outer = lax.ppermute(outer, "dom", others)
    inner = lax.ppermute(inner, "dom", mates)

    far_weights, rest_weights, weights = project(
        jnp.transpose(pattern, (2, 0, 1)), block_counts, exponents, values, matrices, parts, lent
    )
    flat = lambda a: a.reshape(-1, columns)
    far, inner, outer = flat(far), flat(inner), flat(outer)
    send = half_partial("far", far_kernel, far_weights, far)
    send = half_partial(
        "near", functools.partial(near_kernel, far_weights.shape[1]), send, rest_weights, far, inner, outer
    )
    came = lax.ppermute(send, "dom", mates)
    both = came + half_partial("half", half_kernel, weights, far, inner, outer)
    share = terms * columns // parts
    both = both * (1.0 / math.sqrt(row_count * parts))
    both = both.astype(jnp.bfloat16).reshape(parts // 2, share, columns)
    groups = [list(range(core, parts, 2)) for core in range(2)]
    pieces = lax.all_to_all(both, "dom", split_axis=0, concat_axis=0, tiled=True, axis_index_groups=groups)
    summed = jnp.sum(pieces.astype(jnp.float32), axis=0)
    return summed


def solution(mesh):
    return jax.shard_map(
        on_device,
        mesh=mesh,
        in_specs=(
            P(None, ("group", "dom"), None, None, None),
            P(("group", "dom"), None),
            P(("group", "dom")),
            P(None, ("group", "dom"), None),
            P(None, ("group", "dom")),
            P(("group", "dom"), None, None),
            P(("group", "dom"), None),
        ),
        out_specs=P(("group", "dom"), None),
        check_vma=False,
    )
```
